32 devices in a mesh: blk: 4 (over y, x), tok: 8 (over z, core).
Axes of the slice: x: 2, y: 2, z: 4, core: 2. Of those that a mesh axis runs over, the one named last changes fastest.
Arguments:
- tokens: bfloat16 [8, 1024, 1664], P('tok', 'blk'), may hold values from -6 to 6
- segment_ids: int32 [8, 1024], P('tok'), may hold values from 0 to 7, as said below
- merge_index: int32 [8, 256, 4], P('tok'), may hold values from 0 to 1023, as said below
- segment_owner: int32 [8, 8], P('tok'), may hold values from 0 to 7, each once within a row
- ln1_gain: float32 [1664], replicated, may hold values from 0.1 to 1.9
- ln1_bias: float32 [1664], replicated, may hold values from -4 to 4
- w_qkv: bfloat16 [3, 1664, 1664], P(None, 'tok', 'blk'), may hold values from -0.15625 to 0.15625
- qkv_bias: float32 [3, 1664], P(None, 'blk'), may hold values from -6 to 6
- w_out: bfloat16 [1664, 1664], P('blk', 'tok'), may hold values from -0.15625 to 0.15625
- out_bias: float32 [1664], replicated, may hold values from -6 to 6
- ln2_gain: float32 [1664], replicated, may hold values from 0.1 to 1.9
- ln2_bias: float32 [1664], replicated, may hold values from -4 to 4
- w_fc1: bfloat16 [1664, 8192], P(None, 'blk'), may hold values from -0.15625 to 0.15625
- fc1_bias: float32 [8192], P('blk'), may hold values from -6 to 6
- w_fc2: bfloat16 [8192, 1664], P('blk'), may hold values from -0.0625 to 0.0625
- fc2_bias: float32 [1664], replicated, may hold values from -6 to 6
- ln3_gain: float32 [1664], replicated, may hold values from 0.1 to 1.9
- ln3_bias: float32 [1664], replicated, may hold values from -4 to 4
- w_proj: bfloat16 [6656, 1664], P('tok', 'blk'), may hold values from -0.078125 to 0.078125
- proj_bias: float32 [1664], P('blk'), may hold values from -6 to 6
Outputs:
- returned: bfloat16 [8, 8, 64, 1664], P('tok', None, None, 'blk')
The draws below stay inside these ranges and needn't reach their ends.
Inputs may be any that keep to these rules, and one draw needn't show every extreme that they name: `segment_ids`: within a block each segment holds 4 to 256 tokens, one exactly 256; the four tokens of one row of merge_index share a segment. `merge_index`: the rows of one block name each token of the block exactly once. `segment_owner`: each block's row is a permutation of the owners.
All inputs are finite; a program needn't handle non-finite values.
Results may differ from the reference program's by a relative error of at most 0.015.
Values may be sent and summed in bfloat16 or wider, within the bound.
No kernel may reach another device: no remote copies, remote signals or barrier semaphores. Data moves between devices by JAX's collectives and lax.ppermute only.
A program may use at most 128 MiB of HBM per device.

```python
import jax
import jax.numpy as jnp
from jax import lax

D = 1664
HEADS = 16
HD = 104
FF = 8192
TOK_DEV = 1024
MERGED_DEV = 256
SEG_DEV = 8
SLOT = 64
N_TOK = 8


def block_layout(key):
    others_count = SEG_DEV - 1
    spare_units = MERGED_DEV - SLOT - others_count
    base_length = spare_units // others_count
    surplus_units = spare_units - base_length * others_count
    reach_max = max(0, min(base_length, SLOT - 2 - base_length))
    half_count = others_count // 2
    key_order, key_shift, key_pairs, key_place, key_tokens = jax.random.split(key, 5)
    token_shuffle = jax.random.permutation(key_order, others_count)
    extra_allotment = (token_shuffle < surplus_units).astype(jnp.int32)
    shifts = jax.random.randint(key_shift, (half_count,), 0, reach_max + 1).astype(jnp.int32)
    pair_grouped = jnp.zeros((others_count,), jnp.int32)
    pair_grouped = pair_grouped.at[0:2 * half_count:2].set(shifts)
    pair_grouped = pair_grouped.at[1:2 * half_count:2].set(-shifts)
    pair_grouped = pair_grouped[jax.random.permutation(key_pairs, others_count)]
    remaining_length = 1 + base_length + extra_allotment + pair_grouped
    special = jax.random.randint(key_place, (), 0, SEG_DEV).astype(jnp.int32)
    seg_index = jnp.arange(SEG_DEV, dtype=jnp.int32)
    source = jnp.clip(seg_index - (seg_index > special).astype(jnp.int32), 0, others_count - 1)
    lengths = jnp.where(seg_index == special, SLOT, remaining_length[source]).astype(jnp.int32)
    seg_ends = jnp.cumsum(lengths)
    quad_index = jnp.arange(MERGED_DEV, dtype=jnp.int32)
    quad_seg = jnp.sum((quad_index[:, None] >= seg_ends[None, :]).astype(jnp.int32), axis=1).astype(jnp.int32)
    token_order = jax.random.permutation(key_tokens, TOK_DEV).astype(jnp.int32)
    merge_rows = token_order.reshape(MERGED_DEV, 4)
    segment_row = jnp.zeros((TOK_DEV,), jnp.int32).at[token_order].set(jnp.repeat(quad_seg, 4))
    return (segment_row, merge_rows)


def all_layouts(key):
    block_keys = jax.random.split(jax.random.fold_in(key, 11), N_TOK)
    return jax.vmap(block_layout)(block_keys)


def draw_segment_ids(key, part):
    return all_layouts(key)[0]


def draw_merge_index(key, part):
    return all_layouts(key)[1]


def level_of(own_key, extent, shards, least, high):
    loudness, own = 1.0, jax.random.fold_in(own_key, 6)
    for dim, shards_of in shards:
        heights = jnp.exp(jax.random.uniform(jax.random.fold_in(own, dim), (shards_of,), jnp.float32, least / len(shards), high / len(shards)))
        loudness = loudness * jnp.repeat(heights, extent[dim] // shards_of).reshape([-1 if axis == dim else 1 for axis in range(len(extent))])
    return loudness


def noise(stream_key, extent, scale, limit, pieces=(), kind=jnp.bfloat16):
    level = level_of(stream_key, extent, pieces, -0.22, 0.18) if pieces else 1.0
    result = jax.random.normal(stream_key, extent, jnp.float32) * scale * level
    return jnp.minimum(jnp.maximum(result, -limit), limit).astype(kind)


def setup_inputs(seed: int = 0) -> dict:
    streams_of = jax.random.split(jax.random.key(seed), 21)
    tokens = noise(streams_of[0], (N_TOK, TOK_DEV, D), 1.0, 6.0, ((0, 8), (1, 4)))
    segment_ids = draw_segment_ids(jax.random.fold_in(streams_of[20], 71), 0)
    merge_index = draw_merge_index(jax.random.fold_in(streams_of[20], 71), 0)
    segment_owner = jax.vmap(lambda own: jax.random.permutation(own, N_TOK))(jax.random.split(streams_of[3], N_TOK)).reshape((N_TOK, SEG_DEV)).astype(jnp.int32)
    ln1_gain = jnp.clip(1.0 + 0.18 * jax.random.normal(streams_of[4], (D,), jnp.float32), 0.1, 1.9)
    ln1_bias = noise(streams_of[5], (D,), 0.3, 4.0, (), jnp.float32)
    w_qkv = noise(streams_of[6], (3, D, D), D ** -0.5, 0.15625, ((1, 8), (2, 4)))
    qkv_bias = noise(streams_of[7], (3, D), 0.5, 6.0, ((1, 4),), jnp.float32)
    w_out = noise(streams_of[8], (D, D), D ** -0.5, 0.15625, ((0, 4), (1, 8)))
    out_bias = noise(streams_of[9], (D,), 0.5, 6.0, (), jnp.float32)
    ln2_gain = jnp.clip(1.0 + 0.18 * jax.random.normal(streams_of[10], (D,), jnp.float32), 0.1, 1.9)
    ln2_bias = noise(streams_of[11], (D,), 0.3, 4.0, (), jnp.float32)
    w_fc1 = noise(streams_of[12], (D, FF), D ** -0.5, 0.15625, ((1, 4),))
    fc1_bias = noise(streams_of[13], (FF,), 0.5, 6.0, ((0, 4),), jnp.float32)
    w_fc2 = noise(streams_of[14], (FF, D), FF ** -0.5, 0.0625, ((0, 4),))
    fc2_bias = noise(streams_of[15], (D,), 0.5, 6.0, (), jnp.float32)
    ln3_gain = jnp.clip(1.0 + 0.18 * jax.random.normal(streams_of[16], (D,), jnp.float32), 0.1, 1.9)
    ln3_bias = noise(streams_of[17], (D,), 0.3, 4.0, (), jnp.float32)
    w_proj = noise(streams_of[18], (4 * D, D), (4 * D) ** -0.5, 0.078125, ((0, 8), (1, 4)))
    proj_bias = noise(streams_of[19], (D,), 0.5, 6.0, ((0, 4),), jnp.float32)
    return {"tokens": tokens, "segment_ids": segment_ids, "merge_index": merge_index, "segment_owner": segment_owner, "ln1_gain": ln1_gain, "ln1_bias": ln1_bias, "w_qkv": w_qkv, "qkv_bias": qkv_bias, "w_out": w_out, "out_bias": out_bias, "ln2_gain": ln2_gain, "ln2_bias": ln2_bias, "w_fc1": w_fc1, "fc1_bias": fc1_bias, "w_fc2": w_fc2, "fc2_bias": fc2_bias, "ln3_gain": ln3_gain, "ln3_bias": ln3_bias, "w_proj": w_proj, "proj_bias": proj_bias}


EPS = 1e-06

def layer_norm(input_tensors, scales, offset):
    input_tensors = input_tensors.astype(jnp.float32)
    center = input_tensors - lax.optimization_barrier(jnp.mean(input_tensors, axis=-1, keepdims=True))
    spread = lax.optimization_barrier(jnp.mean(center * center, axis=-1, keepdims=True))
    return center * lax.rsqrt(spread + EPS) * scales + offset

def rounded(input_tensors):
    return lax.optimization_barrier(input_tensors.astype(jnp.bfloat16)).astype(jnp.float32)

def reference(tokens, segment_ids, merge_index, segment_owner, ln1_gain, ln1_bias, w_qkv, qkv_bias, w_out, out_bias, ln2_gain, ln2_bias, w_fc1, fc1_bias, w_fc2, fc2_bias, ln3_gain, ln3_bias, w_proj, proj_bias):
    score_scale = 1.0 / HD ** 0.5

    def encode_block(input_tensors):
        tok_block, segment_row, merge_rows, owners_here = input_tensors
        normed_one = rounded(layer_norm(tok_block, ln1_gain, ln1_bias))
        projected_qkv = jnp.einsum('td,cde->cte', normed_one, w_qkv.astype(jnp.float32)) + qkv_bias[:, None, :]
        projected_qkv = rounded(projected_qkv).reshape(3, TOK_DEV, HEADS, HD)
        queries, key_rows, values = (projected_qkv[0], projected_qkv[1], projected_qkv[2])
        scores = jnp.einsum('qhe,khe->hqk', queries, key_rows) * score_scale
        allowed = segment_row[:, None] == segment_row[None, :]
        weights = jnp.where(allowed[None], jnp.exp(scores), 0.0)
        attn_probs = rounded(weights / lax.optimization_barrier(jnp.sum(weights, axis=-1, keepdims=True)))
        attended = jnp.einsum('hqk,khe->qhe', attn_probs, values).reshape(TOK_DEV, D)
        attended = attended.astype(jnp.bfloat16)
        after_attn = tok_block.astype(jnp.float32) + jnp.dot(attended, w_out, preferred_element_type=jnp.float32) + out_bias
        normed_two = layer_norm(after_attn, ln2_gain, ln2_bias).astype(jnp.bfloat16)
        pre_act = jnp.dot(normed_two, w_fc1, preferred_element_type=jnp.float32) + fc1_bias
        hidden_act = jax.nn.gelu(pre_act, approximate=False).astype(jnp.bfloat16)
        layer_out = (after_attn + jnp.dot(hidden_act, w_fc2, preferred_element_type=jnp.float32) + fc2_bias).astype(jnp.bfloat16)
        final_norm = layer_norm(layer_out, ln3_gain, ln3_bias).astype(jnp.bfloat16)
        merged = jnp.take(final_norm, merge_rows.reshape(-1), axis=0).reshape(MERGED_DEV, 4 * D)
        projected = (jnp.dot(merged, w_proj, preferred_element_type=jnp.float32) + proj_bias).astype(jnp.bfloat16)
        seg_rows = jnp.take(segment_row, merge_rows[:, 0])
        seg_match = (seg_rows[:, None] == jnp.arange(SEG_DEV, dtype=jnp.int32)[None, :]).astype(jnp.int32)
        owner_rows = lax.optimization_barrier(jnp.sum(seg_match * owners_here[None, :], axis=1)).astype(jnp.int32)
        segment_matches = (owner_rows[:, None] == jnp.arange(N_TOK, dtype=jnp.int32)[None, :]).astype(jnp.int32)
        before = jnp.cumsum(segment_matches, axis=0) - segment_matches
        order_in = lax.optimization_barrier(jnp.sum(before * segment_matches, axis=1)).astype(jnp.int32)
        return (projected, owner_rows, order_in)
    projected, owner_rows, order_in = lax.map(encode_block, (tokens, segment_ids, merge_index, segment_owner))
    source = jnp.broadcast_to(jnp.arange(N_TOK, dtype=jnp.int32)[:, None], owner_rows.shape)
    returned = jnp.zeros((N_TOK, N_TOK, SLOT, D), jnp.bfloat16)
    return returned.at[owner_rows, source, order_in].set(projected)
```

```python
import functools
import math

import jax
import jax.numpy as jnp
from jax import lax
from jax.experimental import pallas as pl
from jax.experimental.pallas import tpu as pltpu
from jax.sharding import PartitionSpec as P

HD = 104
EPS = 1e-06
BF16 = jnp.bfloat16
F32 = jnp.float32
VMEM_LIMIT = 58 * 1024 * 1024
VM = pl.BlockSpec(memory_space=pltpu.VMEM)
SM = pl.BlockSpec(memory_space=pltpu.SMEM)
ANY = pl.BlockSpec(memory_space=pl.ANY)


def cost(flops, nbytes, trans=0):
    return pl.CostEstimate(flops=int(flops), bytes_accessed=int(nbytes), transcendentals=int(trans))


def params():
    return pltpu.CompilerParams(vmem_limit_bytes=VMEM_LIMIT)


def norm(x, gain, bias):
    center = x - jnp.mean(x, axis=-1, keepdims=True)
    spread = jnp.mean(center * center, axis=-1, keepdims=True)
    return center * lax.rsqrt(spread + EPS) * gain + bias


def swap(x, axis, mask):
    return lax.ppermute(x, axis, [(i, i ^ mask) for i in range(lax.axis_size(axis))])


def unxor(parts, index):
    bit = 1
    while bit < len(parts):
        hit = (index & bit) != 0
        parts = [jnp.where(hit, parts[i ^ bit], parts[i]) for i in range(len(parts))]
        bit *= 2
    return parts


def gather_blk(x):
    half = x.shape[0] // 2
    a, b = x[:half], x[half:]
    xa, yb = swap(a, "blk", 1), swap(b, "blk", 2)
    xb, ya = swap(b, "blk", 1), swap(a, "blk", 2)
    da, db = swap(xa, "blk", 2), swap(yb, "blk", 1)
    return jnp.concatenate([x, xa, xb, ya, yb, da, db], axis=0)


def same_core_groups(count):
    return [list(range(core, count, 2)) for core in range(2)]


def permute_norm_kernel(perm, place, tok, gain, bias, moved, normed):
    pick = (perm[...] == place[...]).astype(F32).astype(BF16)
    rows = jnp.dot(pick, tok[...], preferred_element_type=F32)
    moved[...] = rows.astype(BF16)
    normed[...] = norm(rows, gain[...], bias[...]).astype(BF16)


def permute_norm(perm, place, tok, gain, bias):
    rows, width = tok.shape
    step = 256
    return pl.pallas_call(
        permute_norm_kernel,
        grid=(rows // step,),
        in_specs=[
            pl.BlockSpec((step, 1), lambda i: (i, 0)),
            pl.BlockSpec((1, rows), lambda i: (0, 0)),
            pl.BlockSpec((rows, width), lambda i: (0, 0)),
            pl.BlockSpec((1, width), lambda i: (0, 0)),
            pl.BlockSpec((1, width), lambda i: (0, 0)),
        ],
        out_specs=[pl.BlockSpec((step, width), lambda i: (i, 0))] * 2,
        out_shape=[jax.ShapeDtypeStruct((rows, width), BF16)] * 2,
        compiler_params=params(),
        cost_estimate=cost(2 * rows * rows * width, 6 * rows * width),
        name="permute_norm",
    )(perm, place, tok, gain, bias)


def qkv_kernel(core, h, own, other, bias, out, weight, sems):
    groups, _, shard, _ = own.shape
    me = core[0]
    copies = []
    for z in range(groups):
        for n, (src, c) in enumerate(((own, me), (other, 1 - me))):
            start = pl.multiple_of((2 * z + c) * shard, 16)
            copy = pltpu.make_async_copy(src.at[z], weight.at[:, pl.ds(start, shard), :], sems.at[n, z])
            copy.start()
            copies.append(copy)
    for copy in copies:
        copy.wait()
    rows = h.shape[0]
    step = 256

    for part in range(3):

        @pl.loop(0, rows // step)
        def _(i):
            at = pl.ds(pl.multiple_of(i * step, step), step)
            acc = jnp.dot(h[at, :], weight[part], preferred_element_type=F32)
            out[part, at, :] = (acc + bias[part : part + 1, :]).astype(BF16)


def qkv_project(core, h, own, other, bias):
    groups, parts, shard, cols = own.shape
    rows, width = h.shape
    return pl.pallas_call(
        qkv_kernel,
        in_specs=[SM, VM, ANY, ANY, VM],
        out_specs=VM,
        out_shape=jax.ShapeDtypeStruct((parts, rows, cols), BF16),
        scratch_shapes=[
            pltpu.VMEM((parts, width, cols), BF16),
            pltpu.SemaphoreType.DMA((2, groups)),
        ],
        compiler_params=params(),
        cost_estimate=cost(2 * rows * width * parts * cols, 12e6),
        name="qkv_project",
    )(core, h, own, other, bias)


def attend_kernel(first, step, qkv, row_owner, col_owner, out):
    rows, cols = out.shape
    scale = math.log2(math.e) / math.sqrt(HD)
    keys = qkv.shape[1]
    for head in range(cols // HD):
        at = slice(head * HD, head * HD + HD)
        key = qkv[1, :, at]
        value = jnp.concatenate([qkv[2, :, at], jnp.ones((keys, 128 - HD), BF16)], axis=1)

        @pl.loop(0, rows // step)
        def _(i):
            mine = pl.ds(pl.multiple_of(i * step, step), step)
            query = qkv[0, pl.ds(pl.multiple_of(first + i * step, step), step), at]
            scores = lax.dot_general(query, key, (((1,), (1,)), ((), ())), preferred_element_type=F32)
            kept = row_owner[mine, :] == col_owner[...]
            weights = jnp.where(kept, jnp.exp2(scores * scale), 0.0).astype(BF16)
            mixed = jnp.dot(weights, value, preferred_element_type=F32)
            out[mine, at] = (mixed[:, :HD] / mixed[:, HD : HD + 1]).astype(BF16)


def attend(first, rows, qkv, row_owner, col_owner):
    _, keys, cols = qkv.shape
    return pl.pallas_call(
        functools.partial(attend_kernel, first, 256),
        in_specs=[VM] * 3,
        out_specs=VM,
        out_shape=jax.ShapeDtypeStruct((rows, cols), BF16),
        compiler_params=params(),
        cost_estimate=cost(4 * rows * keys * cols, 4e6, rows * keys * (cols // HD)),
        name="attend",
    )(qkv, row_owner, col_owner)


def mlp_kernel(
    where, att0, att1, att2, att3, tok, wo_own, wo_other, out_bias, gain, bias, w1, b1, w2, b2,
    mine, to1, to2, to3,
    wo, w1v, w2v, after, acc, sems_o, sems_1, sems_2,
):
    core, me = where[0], where[1]
    groups, shard, width = wo_own.shape
    tiles = sems_1.shape[0]
    tile = w1.shape[1] // tiles
    quarter = mine.shape[1]
    loads_o, loads_1, loads_2 = [], [], []
    for r in range(groups):
        for n, (src, c) in enumerate(((wo_own, core), (wo_other, 1 - core))):
            start = pl.multiple_of((2 * r + c) * shard, 16)
            loads_o.append(pltpu.make_async_copy(src.at[r], wo.at[pl.ds(start, shard), :], sems_o.at[n, r]))
    for t in range(tiles):
        at = slice(t * tile, t * tile + tile)
        loads_1.append(pltpu.make_async_copy(w1.at[:, at], w1v.at[:, at], sems_1.at[t]))
        loads_2.append(pltpu.make_async_copy(w2.at[at, :], w2v.at[at, :], sems_2.at[t]))
    for copy in loads_o:
        copy.start()
    for first, second in zip(loads_1, loads_2):
        first.start()
        second.start()
    for copy in loads_o:
        copy.wait()
    depth = 2 * shard
    total = tok[...].astype(F32) + out_bias[...]
    for r, att in enumerate((att0, att1, att2, att3)):
        total = total + jnp.dot(att[...], wo[r * depth : r * depth + depth, :], preferred_element_type=F32)
    after[...] = total
    h = norm(total, gain[...], bias[...]).astype(BF16)
    for t in range(tiles):
        at = slice(t * tile, t * tile + tile)
        loads_1[t].wait()
        pre = jnp.dot(h, w1v[:, at], preferred_element_type=F32) + b1[:, at]
        hidden = (0.5 * pre * (1.0 + lax.erf(pre * math.sqrt(0.5)))).astype(BF16)
        loads_2[t].wait()
        part = jnp.dot(hidden, w2v[at, :], preferred_element_type=F32)
        if t == 0:
            acc[...] = part
        else:
            acc[...] += part
    for place in range(4):

        @pl.when(me == place)
        def _(place=place):
            at = slice(place * quarter, place * quarter + quarter)
            mine[...] = acc[:, at] + after[:, at] + b2[:, at]
            for r, ref in ((1, to1), (2, to2), (3, to3)):
                first = (place ^ r) * quarter
                ref[...] = acc[:, first : first + quarter].astype(BF16)


def mlp(where, atts, tok, wo_own, wo_other, out_bias, gain, bias, w1, b1, w2, b2):
    rows, width = tok.shape
    groups, shard, _ = wo_own.shape
    hidden = w1.shape[1]
    quarter = width // 4
    tiles = 4
    return pl.pallas_call(
        mlp_kernel,
        in_specs=[SM, VM, VM, VM, VM, VM, ANY, ANY, VM, VM, VM, ANY, VM, ANY, VM],
        out_specs=[VM] * 4,
        out_shape=[jax.ShapeDtypeStruct((rows, quarter), F32)]
        + [jax.ShapeDtypeStruct((rows, quarter), BF16)] * 3,
        scratch_shapes=[
            pltpu.VMEM((2 * groups * shard, width), BF16),
            pltpu.VMEM(w1.shape, BF16),
            pltpu.VMEM(w2.shape, BF16),
            pltpu.VMEM((rows, width), F32),
            pltpu.VMEM((rows, width), F32),
            pltpu.SemaphoreType.DMA((2, groups)),
            pltpu.SemaphoreType.DMA((tiles,)),
            pltpu.SemaphoreType.DMA((tiles,)),
        ],
        compiler_params=params(),
        cost_estimate=cost(2 * rows * width * (width + 2 * hidden), 25e6, rows * hidden),
        name="out_mlp",
    )(where, *atts, tok, wo_own, wo_other, out_bias, gain, bias, w1, b1, w2, b2)


def project_kernel(where, layer, stats, gain, bias, wp_own, wp_other, mine, to1, to2, to3, wp, acc, sems):
    core, me = where[0], where[1]
    folds, shard, width = wp_own.shape
    quarter = mine.shape[1]
    count = mine.shape[0]
    copies = []
    for k in range(folds):
        for n, (src, c) in enumerate(((wp_own, core), (wp_other, 1 - core))):
            start = pl.multiple_of((2 * k + c) * shard, 16)
            copies.append(pltpu.make_async_copy(src.at[k], wp.at[pl.ds(start, shard), :], sems.at[n, k]))
    for copy in copies:
        copy.start()
    scale, shift = stats[:, 0:1], stats[:, 1:2]
    final = ((layer[...].astype(F32) - shift) * scale * gain[...] + bias[...]).astype(BF16)
    for copy in copies:
        copy.wait()
    depth = 2 * shard
    for k in range(folds):
        part = jnp.dot(
            final[k * count : k * count + count], wp[k * depth : k * depth + depth, :], preferred_element_type=F32
        )
        if k == 0:
            acc[...] = part
        else:
            acc[...] += part
    for place in range(4):

        @pl.when(me == place)
        def _(place=place):
            at = slice(place * quarter, place * quarter + quarter)
            mine[...] = acc[:, at]
            for r, ref in ((1, to1), (2, to2), (3, to3)):
                first = (place ^ r) * quarter
                ref[...] = acc[:, first : first + quarter].astype(BF16)


def project(where, layer, stats, gain, bias, wp_own, wp_other):
    folds, shard, width = wp_own.shape
    count = layer.shape[0] // folds
    quarter = width // 4
    return pl.pallas_call(
        project_kernel,
        in_specs=[SM, VM, VM, VM, VM, ANY, ANY],
        out_specs=[VM] * 4,
        out_shape=[jax.ShapeDtypeStruct((count, quarter), F32)]
        + [jax.ShapeDtypeStruct((count, quarter), BF16)] * 3,
        scratch_shapes=[
            pltpu.VMEM((2 * folds * shard, width), BF16),
            pltpu.VMEM((count, width), F32),
            pltpu.SemaphoreType.DMA((2, folds)),
        ],
        compiler_params=params(),
        cost_estimate=cost(2 * count * folds * 2 * shard * width, 7e6),
        name="project",
    )(where, layer, stats, gain, bias, wp_own, wp_other)


def gather_qkv(w_qkv, core):
    parts, shard, cols = w_qkv.shape
    count = lax.axis_size("tok")
    if shard % 16:
        whole = lax.all_gather(w_qkv, "tok", axis=1, tiled=True)
        low, high = whole[None, :, : whole.shape[1] // 2], whole[None, :, whole.shape[1] // 2 :]
        return jnp.where(core == 0, low, high), jnp.where(core == 0, high, low)
    own = lax.all_gather(
        w_qkv.reshape(parts * shard, cols), "tok", axis=0, tiled=True, axis_index_groups=same_core_groups(count)
    ).reshape(count // 2, parts, shard, cols)
    return own, swap(own, "tok", 1)


def gather_out(w_out, core, tok):
    depth, shard = w_out.shape
    count = lax.axis_size("tok")
    near = jnp.stack([w_out] + [swap(w_out, "tok", 2 * s) for s in range(1, count // 2)])
    far = swap(near, "tok", 1)
    slots = [(near if s % 2 == 0 else far)[s // 2] for s in range(count)]
    whole = jnp.concatenate(unxor(slots, tok), axis=1)
    half = depth // 2
    part = jnp.where(core == 0, whole[:half], whole[half:])
    own = gather_blk(part).reshape(4, half, whole.shape[1])
    return own, swap(own, "tok", 1)


def gather_proj(w_proj, core, blk):
    rows, quarter = w_proj.shape
    count = lax.axis_size("tok")
    width = 4 * quarter
    half = quarter // 2
    if rows == 2 * quarter and count == 8:
        halves = w_proj.reshape(2, 2, half, quarter)
        keep = jnp.where(core == 0, halves[:, 0], halves[:, 1])
        give = jnp.where(core == 0, halves[:, 1], halves[:, 0])
        got = swap(give, "tok", 1)
        low = jnp.where(core == 0, keep, got)
        high = jnp.where(core == 0, got, keep)
        pieces = unxor([low[0], low[1], high[0], high[1]], blk)
        pieces = [pieces[0]] + [swap(pieces[r], "blk", r) for r in range(1, 4)]
        mine = jnp.concatenate(unxor(pieces, blk), axis=1)
        own = lax.all_gather(mine, "tok", axis=0, tiled=True, axis_index_groups=same_core_groups(count))
        own = own.reshape(4, half, width)
        return own, swap(own, "tok", 1)
    whole = lax.all_gather(w_proj, "tok", axis=0, tiled=True).reshape(4, 4, quarter, quarter)
    whole = lax.all_to_all(whole, "blk", split_axis=1, concat_axis=3, tiled=True)
    whole = whole.reshape(4, 2, half, width)
    low, high = whole[:, 0], whole[:, 1]
    return jnp.where(core == 0, low, high), jnp.where(core == 0, high, low)


def body(
    tokens,
    segment_ids,
    merge_index,
    segment_owner,
    ln1_gain,
    ln1_bias,
    w_qkv,
    qkv_bias,
    w_out,
    out_bias,
    ln2_gain,
    ln2_bias,
    w_fc1,
    fc1_bias,
    w_fc2,
    fc2_bias,
    ln3_gain,
    ln3_bias,
    w_proj,
    proj_bias,
):
    blk, tok = lax.axis_index("blk"), lax.axis_index("tok")
    core = tok % 2
    tok_count = lax.axis_size("tok")
    where = jnp.stack([core, blk]).astype(jnp.int32)
    block = tokens[0]
    local_rows, width = block.shape
    rows = 4 * local_rows
    quarter = width // 4
    merges = merge_index[0]
    merged_count, folds = merges.shape

    gathered = gather_blk(block)
    qkv_own, qkv_other = gather_qkv(w_qkv, core)
    out_own, out_other = gather_out(w_out, core, tok)
    proj_own, proj_other = gather_proj(w_proj, core, blk)

    ids = jnp.arange(rows, dtype=jnp.int32)
    seg_of = jnp.sum(jnp.where(merges[:, :1] == ids[None, :], segment_ids[0][None, :], 0), axis=1)
    owners = segment_owner[0]
    owner = jnp.sum(
        jnp.where(seg_of[:, None] == jnp.arange(owners.shape[0], dtype=jnp.int32)[None, :], owners[None, :], 0),
        axis=1,
    )
    order = jnp.arange(merged_count, dtype=jnp.int32)
    ahead = (owner[None, :] < owner[:, None]) | ((owner[None, :] == owner[:, None]) & (order[None, :] < order[:, None]))
    place = jnp.sum(ahead.astype(jnp.int32), axis=1)
    at_place = place[None, :] == order[:, None]
    owner_sorted = jnp.sum(jnp.where(at_place, owner[None, :], 0), axis=1)
    merges_sorted = jnp.sum(jnp.where(at_place[:, :, None], merges[None, :, :], 0), axis=1)
    chunks = 2
    count = merged_count // chunks
    perm = merges_sorted.reshape(chunks, count, folds).transpose(0, 2, 1).reshape(rows, 1)
    row_owner = jnp.broadcast_to(owner_sorted.reshape(chunks, 1, count), (chunks, folds, count)).reshape(rows)
    source = ((ids // local_rows) ^ blk) * local_rows + ids % local_rows

    moved, normed = permute_norm(perm, source[None, :], gathered, ln1_gain[None, :], ln1_bias[None, :])
    qkv = qkv_project(where, normed, qkv_own, qkv_other, qkv_bias)

    chunk_rows = rows // chunks
    layers = []
    for n in range(chunks):
        at = slice(n * chunk_rows, n * chunk_rows + chunk_rows)
        att = attend(n * chunk_rows, chunk_rows, qkv, row_owner[at, None], row_owner[None, :])
        atts = [att] + [swap(att, "blk", r) for r in range(1, 4)]
        own, *sends = mlp(
            where, atts, moved[at], out_own, out_other, out_bias[None, :], ln2_gain[None, :], ln2_bias[None, :],
            w_fc1, fc1_bias[None, :], w_fc2, fc2_bias[None, :],
        )
        for r in range(1, 4):
            own = own + swap(sends[r - 1], "blk", r).astype(F32)
        layers.append(own.astype(BF16))

    gain3 = lax.dynamic_slice_in_dim(ln3_gain, blk * quarter, quarter, 0)
    bias3 = lax.dynamic_slice_in_dim(ln3_bias, blk * quarter, quarter, 0)
    outs = []
    for layer in layers:
        wide = layer.astype(F32)
        mean = jnp.mean(wide, axis=-1)
        centered = wide - mean[:, None]
        stat = jnp.stack([mean, jnp.sum(centered * centered, axis=-1)])
        stat = [stat] + [swap(stat, "blk", r) for r in range(1, 4)]
        means = [s[0] for s in stat]
        mean = sum(means) * 0.25
        spread = sum(s[1] for s in stat) + quarter * sum((m - mean) ** 2 for m in means)
        stats = jnp.stack([lax.rsqrt(spread / width + EPS), mean], axis=1)
        own, *sends = project(where, layer, stats, gain3[None, :], bias3[None, :], proj_own, proj_other)
        for r in range(1, 4):
            own = own + swap(sends[r - 1], "blk", r).astype(F32)
        outs.append((own + proj_bias[None, :]).astype(BF16))
    projected = jnp.concatenate(outs, axis=0)

    slot_cap = 2 * merged_count // tok_count
    first = jnp.sum((owner_sorted[None, :] < owner_sorted[:, None]).astype(jnp.int32), axis=1)
    target = owner_sorted * slot_cap + order - first
    placed = (jnp.arange(tok_count * slot_cap, dtype=jnp.int32)[:, None] == target[None, :]).astype(BF16)
    outgoing = jnp.dot(placed, projected, preferred_element_type=F32).astype(BF16)
    outgoing = outgoing.reshape(tok_count, slot_cap, projected.shape[1])
    arrived = lax.all_to_all(outgoing, "tok", split_axis=0, concat_axis=0, tiled=True)
    return arrived[None]


def solution(mesh):
    placed = (
        P("tok", "blk", None),
        P("tok", None),
        P("tok", None, None),
        P("tok", None),
        P(),
        P(),
        P(None, "tok", "blk"),
        P(None, "blk"),
        P("blk", "tok"),
        P(),
        P(),
        P(),
        P(None, "blk"),
        P("blk"),
        P("blk", None),
        P(),
        P(),
        P(),
        P("tok", "blk"),
        P("blk"),
    )
    return jax.shard_map(
        body, mesh=mesh, in_specs=placed, out_specs=P("tok", None, None, "blk"), check_vma=False
    )
```

```python
import functools
import math

import jax
import jax.numpy as jnp
from jax import lax
from jax.experimental import pallas as pl
from jax.experimental.pallas import tpu as pltpu
from jax.sharding import PartitionSpec as P

HD = 104
EPS = 1e-06
CHUNKS = 2
BF16 = jnp.bfloat16
F32 = jnp.float32
VM = pl.BlockSpec(memory_space=pltpu.VMEM)
SM = pl.BlockSpec(memory_space=pltpu.SMEM)
ANY = pl.BlockSpec(memory_space=pl.ANY)


def cost(flops, nbytes, trans=0):
    return pl.CostEstimate(flops=int(flops), bytes_accessed=int(nbytes), transcendentals=int(trans))


def params(mib):
    return pltpu.CompilerParams(vmem_limit_bytes=mib * 1024 * 1024)


def norm(x, gain, bias):
    center = x - jnp.mean(x, axis=-1, keepdims=True)
    spread = jnp.mean(center * center, axis=-1, keepdims=True)
    return center * lax.rsqrt(spread + EPS) * gain + bias


def swap(x, axis, mask):
    return lax.ppermute(x, axis, [(i, i ^ mask) for i in range(lax.axis_size(axis))])


def stage(*arrays):
    return lax.optimization_barrier(arrays)


def same_core_groups(count):
    return [list(range(core, count, 2)) for core in range(2)]


def permute_norm_kernel(count, perm, place, gain, bias, *refs):
    pieces, (moved, normed, tok, sems) = refs[:count], refs[count:]

    @pl.when(pl.program_id(0) == 0)
    def _():
        copies, start = [], 0
        for n, piece in enumerate(pieces):
            size = piece.shape[0]
            copies.append(pltpu.make_async_copy(piece, tok.at[pl.ds(start, size), :], sems.at[n]))
            start += size
        for copy in copies:
            copy.start()
        for copy in copies:
            copy.wait()

    pick = (perm[...] == place[...]).astype(F32).astype(BF16)
    rows = jnp.dot(pick, tok[...], preferred_element_type=F32)
    moved[...] = rows.astype(BF16)
    normed[...] = norm(rows, gain[...], bias[...]).astype(BF16)


def permute_norm(perm, place, pieces, gain, bias):
    rows, width = perm.shape[0], pieces[0].shape[1]
    step = 256
    return pl.pallas_call(
        functools.partial(permute_norm_kernel, len(pieces)),
        grid=(rows // step,),
        in_specs=[
            pl.BlockSpec((step, 1), lambda i: (i, 0)),
            pl.BlockSpec((1, rows), lambda i: (0, 0)),
            pl.BlockSpec((1, width), lambda i: (0, 0)),
            pl.BlockSpec((1, width), lambda i: (0, 0)),
        ]
        + [ANY] * len(pieces),
        out_specs=[pl.BlockSpec((step, width), lambda i: (i, 0))] * 2,
        out_shape=[jax.ShapeDtypeStruct((rows, width), BF16)] * 2,
        scratch_shapes=[pltpu.VMEM((rows, width), BF16), pltpu.SemaphoreType.DMA((len(pieces),))],
        compiler_params=params(56),
        cost_estimate=cost(2 * rows * rows * width, 6 * rows * width),
        name="permute_norm",
    )(perm, place, gain, bias, *pieces)


def transpose_kernel(x, out):
    out[...] = x[...].T


def transpose(x):
    return pl.pallas_call(
        transpose_kernel,
        in_specs=[VM],
        out_specs=VM,
        out_shape=jax.ShapeDtypeStruct(x.shape[::-1], x.dtype),
        compiler_params=params(8),
        cost_estimate=cost(0, 4 * x.size),
        name="transpose",
    )(x)


def qkv_kernel(core, h, own, other, bias, out, weight, sems):
    groups, _, shard, _ = own.shape
    me = core[0]
    copies = []
    for z in range(groups):
        for n, (src, c) in enumerate(((own, me), (other, 1 - me))):
            start = pl.multiple_of((2 * z + c) * shard, 16)
            copy = pltpu.make_async_copy(src.at[z], weight.at[:, pl.ds(start, shard), :], sems.at[n, z])
            copy.start()
            copies.append(copy)
    for copy in copies:
        copy.wait()
    rows = h.shape[0]
    step = 256

    for part in range(3):

        @pl.loop(0, rows // step)
        def _(i):
            at = pl.ds(pl.multiple_of(i * step, step), step)
            acc = jnp.dot(h[at, :], weight[part], preferred_element_type=F32)
            out[part, at, :] = (acc + bias[part : part + 1, :]).astype(BF16)


def qkv_project(core, h, own, other, bias):
    groups, parts, shard, cols = own.shape
    rows, width = h.shape
    return pl.pallas_call(
        qkv_kernel,
        in_specs=[SM, VM, ANY, ANY, VM],
        out_specs=VM,
        out_shape=jax.ShapeDtypeStruct((parts, rows, cols), BF16),
        scratch_shapes=[
            pltpu.VMEM((parts, width, cols), BF16),
            pltpu.SemaphoreType.DMA((2, groups)),
        ],
        compiler_params=params(24),
        cost_estimate=cost(2 * rows * width * parts * cols, 12e6),
        name="qkv_project",
    )(core, h, own, other, bias)


def attend_kernel(first, qkv, row_owner, col_owner, *outs):
    cols, step = outs[0].shape
    scale = math.log2(math.e) / math.sqrt(HD)
    keys = qkv.shape[1]
    for head in range(cols // HD):
        at = slice(head * HD, head * HD + HD)
        key = qkv[1, :, at]
        value = jnp.concatenate([qkv[2, :, at], jnp.ones((keys, 128 - HD), BF16)], axis=1)
        for n, out in enumerate(outs):
            start = n * step
            mine = slice(start, start + step)
            query = qkv[0, first + start : first + start + step, at]
            scores = lax.dot_general(query, key, (((1,), (1,)), ((), ())), preferred_element_type=F32)
            kept = row_owner[mine, :] == col_owner[...]
            weights = jnp.where(kept, jnp.exp2(scores * scale), 0.0).astype(BF16)
            mixed = jnp.dot(weights, value, preferred_element_type=F32)
            out[at, :] = (mixed / mixed[:, HD : HD + 1]).T[:HD, :].astype(BF16)


def attend(first, rows, qkv, row_owner, col_owner):
    _, keys, cols = qkv.shape
    return pl.pallas_call(
        functools.partial(attend_kernel, first),
        in_specs=[VM] * 3,
        out_specs=[VM] * 2,
        out_shape=[jax.ShapeDtypeStruct((cols, rows // 2), BF16)] * 2,
        compiler_params=params(16),
        cost_estimate=cost(4 * rows * keys * cols, 4e6, rows * keys * (cols // HD)),
        name="attend",
    )(qkv, row_owner, col_owner)


def mlp_kernel(first, where, out_bias, gain, bias, b1, b2, tok, w1, w2, *refs):
    atts, wos, (mine, to1, to2, to3, *scratch) = refs[:4], refs[4:6], refs[6:]
    tok_in, att_in, w1_in, w2_in, wo, total, h, hidden, sem_a, sem_o, sem_w = scratch
    core, me = where[0], where[1]
    quarter, rows = mine.shape
    step = rows // 2
    early = [pltpu.make_async_copy(tok.at[first : first + rows, :], tok_in, sem_a.at[4])]
    for n, src in enumerate(atts):
        early.append(pltpu.make_async_copy(src, att_in.at[n], sem_a.at[n]))
    count, slots = wos[0].shape[1], sem_o.shape[2]
    size = min(count, wo.shape[1] // 2 // slots)
    for n, src in enumerate(wos):
        for m, r in enumerate((0, 1, 2, 3, 0, 2, 1, 3)):
            for p in range(count // size):
                row = (m // 4) * count + p * size
                slot, off = divmod(row, wo.shape[1] // 2 // slots)
                place = (where[2] ^ (2 * slot) ^ n) * (wo.shape[1] // 2 // slots) + off
                start = pl.multiple_of(place, 16)
                early.append(
                    pltpu.make_async_copy(
                        src.at[m, p * size : p * size + size, :],
                        wo.at[r, pl.ds(start, size), :],
                        sem_o.at[n, m, p],
                    )
                )
    parts = sem_w.shape[1]
    late = []
    for n, (src, dst) in enumerate(((w1, w1_in), (w2, w2_in))):
        size = src.shape[0] // parts
        cuts = [slice(p * size, p * size + size) for p in range(parts)]
        late.append(
            [pltpu.make_async_copy(src.at[at, :], dst.at[at, :], sem_w.at[n, p]) for p, at in enumerate(cuts)]
        )
    for copy in early:
        copy.start()
    for copy in early:
        copy.wait()
    for copy in late[0] + late[1]:
        copy.start()

    for n, pairs in enumerate((((0, (0, 1)), (1, (2, 3))), ((2, (0, 2)), (3, (1, 3))))):
        at = slice(n * step, n * step + step)
        summed = tok_in[at, :].astype(F32) + out_bias[...]
        for a, places in pairs:
            for m, r in enumerate(places):
                summed = summed + lax.dot_general(
                    att_in[a, m],
                    wo[r],
                    (((0,), (1,)), ((), ())),
                    preferred_element_type=F32,
                )
        total[at, :] = summed
        h[at, :] = norm(summed, gain[...], bias[...]).astype(BF16)

    for copy in late[0]:
        copy.wait()
    tile = 512

    @pl.loop(0, rows // step)
    def _(i):
        at = pl.ds(pl.multiple_of(i * step, step), step)
        for start in range(0, w1.shape[1], tile):
            cols = slice(start, start + tile)
            pre = jnp.dot(h[at, :], w1_in[:, cols], preferred_element_type=F32) + b1[:, cols]
            hidden[at, cols] = (0.5 * pre * (1.0 + lax.erf(pre * math.sqrt(0.5)))).astype(BF16)

    for place in range(4):

        @pl.when(me == place)
        def _(place=place):
            at = slice(place * quarter, place * quarter + quarter)
            mine[...] = (total[:, at] + b2[:, at]).T

    for copy in late[1]:
        copy.wait()

    @pl.loop(0, rows // step)
    def _(i):
        at = pl.ds(pl.multiple_of(i * step, step), step)
        total[at, :] = jnp.dot(hidden[at, :], w2_in[...], preferred_element_type=F32)

    for place in range(4):

        @pl.when(me == place)
        def _(place=place):
            mine[...] += total[:, place * quarter : place * quarter + quarter].T
            for r, ref in ((1, to1), (2, to2), (3, to3)):
                start = (place ^ r) * quarter
                ref[...] = total[:, start : start + quarter].T.astype(BF16)


def mlp(first, rows, where, slots, atts, wos, tok, out_bias, gain, bias, w1, b1, w2, b2):
    width = tok.shape[1]
    hidden = w1.shape[1]
    quarter = width // 4
    parts = 4
    return pl.pallas_call(
        functools.partial(mlp_kernel, first),
        in_specs=[SM] + [VM] * 5 + [ANY] * (3 + len(atts) + len(wos)),
        out_specs=[VM] * 4,
        out_shape=[jax.ShapeDtypeStruct((quarter, rows), F32)]
        + [jax.ShapeDtypeStruct((quarter, rows), BF16)] * 3,
        scratch_shapes=[
            pltpu.VMEM((rows, width), BF16),
            pltpu.VMEM((len(atts), *atts[0].shape), BF16),
            pltpu.VMEM(w1.shape, BF16),
            pltpu.VMEM(w2.shape, BF16),
            pltpu.VMEM((4, width, quarter), BF16),
            pltpu.VMEM((rows, width), F32),
            pltpu.VMEM((rows, width), BF16),
            pltpu.VMEM((rows, hidden), BF16),
            pltpu.SemaphoreType.DMA((len(atts) + 1,)),
            pltpu.SemaphoreType.DMA((len(wos), 8, slots)),
            pltpu.SemaphoreType.DMA((2, parts)),
        ],
        compiler_params=params(52),
        cost_estimate=cost(2 * rows * width * (width + 2 * hidden), 25e6, rows * hidden),
        name="out_mlp",
    )(where, out_bias, gain, bias, b1, b2, tok, w1, w2, *atts, *wos)


def project_kernel(where, layer, stats, gain, bias, wp_own, wp_other, mine, to1, to2, to3, wp, acc, sems):
    core, me = where[0], where[1]
    folds, shard, width = wp_own.shape
    quarter = mine.shape[0]
    copies = []
    for k in range(folds):
        for n, (src, c) in enumerate(((wp_own, core), (wp_other, 1 - core))):
            start = pl.multiple_of((2 * k + c) * shard, 16)
            copies.append(pltpu.make_async_copy(src.at[k], wp.at[pl.ds(start, shard), :], sems.at[n, k]))
    for copy in copies:
        copy.start()
    scale, shift = stats[0:1, :], stats[1:2, :]
    final = ((layer[...].astype(F32) - shift) * scale * gain[...] + bias[...]).astype(BF16)
    for copy in copies:
        copy.wait()
    depth = 2 * shard
    each = final.shape[1] // folds // CHUNKS
    for n in range(CHUNKS):
        part = 0.0
        for k in range(folds):
            start = (n * folds + k) * each
            part = part + lax.dot_general(
                final[:, start : start + each],
                wp[k * depth : k * depth + depth, :],
                (((0,), (0,)), ((), ())),
                preferred_element_type=F32,
            )
        acc[n * each : n * each + each, :] = part
    for place in range(4):

        @pl.when(me == place)
        def _(place=place):
            at = slice(place * quarter, place * quarter + quarter)
            mine[...] = acc[:, at].T
            for r, ref in ((1, to1), (2, to2), (3, to3)):
                first = (place ^ r) * quarter
                ref[...] = acc[:, first : first + quarter].T.astype(BF16)


def project(where, layer, stats, gain, bias, wp_own, wp_other):
    folds, shard, width = wp_own.shape
    count = layer.shape[1] // folds
    quarter = width // 4
    return pl.pallas_call(
        project_kernel,
        in_specs=[SM, VM, VM, VM, VM, ANY, ANY],
        out_specs=[VM] * 4,
        out_shape=[jax.ShapeDtypeStruct((quarter, count), F32)]
        + [jax.ShapeDtypeStruct((quarter, count), BF16)] * 3,
        scratch_shapes=[
            pltpu.VMEM((2 * folds * shard, width), BF16),
            pltpu.VMEM((count, width), F32),
            pltpu.SemaphoreType.DMA((2, folds)),
        ],
        compiler_params=params(16),
        cost_estimate=cost(2 * count * folds * 2 * shard * width, 7e6),
        name="project",
    )(where, layer, stats, gain, bias, wp_own, wp_other)


def gather_qkv(w_qkv, core):
    parts, shard, cols = w_qkv.shape
    count = lax.axis_size("tok")
    if shard % 16:
        whole = lax.all_gather(w_qkv, "tok", axis=1, tiled=True)
        low, high = whole[None, :, : whole.shape[1] // 2], whole[None, :, whole.shape[1] // 2 :]
        return jnp.where(core == 0, low, high), jnp.where(core == 0, high, low)
    own = lax.all_gather(
        w_qkv.reshape(parts * shard, cols), "tok", axis=0, tiled=True, axis_index_groups=same_core_groups(count)
    ).reshape(count // 2, parts, shard, cols)
    return own, None


def gather_proj_whole(w_proj, core):
    _, quarter = w_proj.shape
    whole = lax.all_gather(w_proj, "tok", axis=0, tiled=True).reshape(4, 4, quarter, quarter)
    whole = lax.all_to_all(whole, "blk", split_axis=1, concat_axis=3, tiled=True)
    whole = whole.reshape(4, 2, quarter // 2, 4 * quarter)
    low, high = whole[:, 0], whole[:, 1]
    return jnp.where(core == 0, low, high), jnp.where(core == 0, high, low)


def body(
    tokens,
    segment_ids,
    merge_index,
    segment_owner,
    ln1_gain,
    ln1_bias,
    w_qkv,
    qkv_bias,
    w_out,
    out_bias,
    ln2_gain,
    ln2_bias,
    w_fc1,
    fc1_bias,
    w_fc2,
    fc2_bias,
    ln3_gain,
    ln3_bias,
    w_proj,
    proj_bias,
):
    blk, tok = lax.axis_index("blk"), lax.axis_index("tok")
    core = tok % 2
    tok_count = lax.axis_size("tok")
    block = tokens[0]
    local_rows, width = block.shape
    rows = 4 * local_rows
    quarter = width // 4
    merges = merge_index[0]
    merged_count, folds = merges.shape

    half = local_rows // 2
    split_proj = w_proj.shape[0] == 2 * quarter and tok_count == 8
    even, low = (blk & 1) == 0, (blk & 2) == 0

    qkv_own, qkv_other = gather_qkv(w_qkv, core)
    a, b = block[:half], block[half:]
    depth, shard = w_out.shape
    if shard % 16:
        whole = lax.all_gather(w_out, "tok", axis=1, tiled=True).T
        shards = [lax.dynamic_slice_in_dim(whole, core * (width // 2), width // 2, 0)]
        where = jnp.stack([core, blk, core]).astype(jnp.int32)
    else:
        shards = [transpose(w_out)]
        shards += [swap(shards[0], "tok", 2 * n) for n in range(1, tok_count // 2)]
        where = jnp.stack([core, blk, tok]).astype(jnp.int32)
    xa, yb = swap(a, "blk", 1), swap(b, "blk", 2)
    xa, yb = stage(xa, yb)

    a, b = jnp.concatenate([a, xa], axis=0), jnp.concatenate([b, yb], axis=0)
    ya, xb = swap(a, "blk", 2), swap(b, "blk", 1)
    if split_proj:
        halves = stage(w_proj, a)[0].reshape(2, 2, quarter // 2, quarter)
        keep = jnp.where(core == 0, halves[:, 0], halves[:, 1])
        got = swap(jnp.where(core == 0, halves[:, 1], halves[:, 0]), "tok", 1)
        near = jnp.where((core == 0) == low, keep, got)
        far = jnp.where((core == 0) == low, got, keep)
        ya, xb, near, far = stage(ya, xb, near, far)
    else:
        ya, xb = stage(ya, xb)
    pieces = [a, ya, b, xb]

    ids = jnp.arange(rows, dtype=jnp.int32)
    seg_of = jnp.sum(jnp.where(merges[:, :1] == ids[None, :], segment_ids[0][None, :], 0), axis=1)
    owners = segment_owner[0]
    owner = jnp.sum(
        jnp.where(seg_of[:, None] == jnp.arange(owners.shape[0], dtype=jnp.int32)[None, :], owners[None, :], 0),
        axis=1,
    )
    order = jnp.arange(merged_count, dtype=jnp.int32)
    ahead = (owner[None, :] < owner[:, None]) | ((owner[None, :] == owner[:, None]) & (order[None, :] < order[:, None]))
    place = jnp.sum(ahead.astype(jnp.int32), axis=1)
    at_place = place[None, :] == order[:, None]
    owner_sorted = jnp.sum(jnp.where(at_place, owner[None, :], 0), axis=1)
    merges_sorted = jnp.sum(jnp.where(at_place[:, :, None], merges[None, :, :], 0), axis=1)
    chunks = CHUNKS
    count = merged_count // chunks
    perm = merges_sorted.reshape(chunks, count, folds).transpose(0, 2, 1).reshape(rows, 1)
    row_owner = jnp.broadcast_to(owner_sorted.reshape(chunks, 1, count), (chunks, folds, count)).reshape(rows)
    nth = ids // half
    swapped = (nth & 1) * 2 + (nth & 2) // 2
    device = jnp.where(nth < 4, nth, swapped) ^ blk
    source = device * local_rows + jnp.where(nth < 4, 0, half) + ids % half

    moved, normed = permute_norm(perm, source[None, :], pieces, ln1_gain[None, :], ln1_bias[None, :])
    if split_proj:
        got = swap(far, "blk", 2)
        moved, normed, got, *shards = stage(moved, normed, got, *shards)
        pair = jnp.concatenate([jnp.where(low, near, got), jnp.where(low, got, near)], axis=2)
        keep, give = jnp.where(even, pair[0], pair[1]), jnp.where(even, pair[1], pair[0])
    else:
        moved, normed, *shards = stage(moved, normed, *shards)

    slots = len(shards)
    shards = jnp.concatenate(shards, axis=0)
    a, b = shards[: width // 4], shards[width // 4 :]
    xa, yb = swap(a, "blk", 1), swap(b, "blk", 2)
    if qkv_other is None:
        qkv_own, normed = stage(qkv_own, normed)
        qkv_other = swap(qkv_own, "tok", 1)
    qkv_own, qkv_other = stage(qkv_own, qkv_other)
    qkv = qkv_project(where, normed, qkv_own, qkv_other, qkv_bias)
    if split_proj:
        got = swap(give, "blk", 1)
        qkv, xa, yb, got = stage(qkv, xa, yb, got)
        one, two = jnp.where(even, keep, got), jnp.where(even, got, keep)
        mine = jnp.concatenate([one[:, :quarter], two[:, :quarter], one[:, quarter:], two[:, quarter:]], axis=1)
        proj_own = lax.all_gather(mine, "tok", axis=0, tiled=True, axis_index_groups=same_core_groups(tok_count))
        proj_own = proj_own.reshape(4, quarter // 2, width)
    else:
        qkv, xa, yb = stage(qkv, xa, yb)
        proj_own, proj_other = gather_proj_whole(w_proj, core)

    chunk_rows = rows // chunks
    a, b = jnp.stack([a, xa]), jnp.stack([b, yb])
    ya, xb = swap(a, "blk", 2), swap(b, "blk", 1)
    a0, b0 = attend(0, chunk_rows, qkv, row_owner[:chunk_rows, None], row_owner[None, :])
    a0, b0, qkv = stage(a0, b0, qkv)

    xa0, yb0 = swap(a0, "blk", 1), swap(b0, "blk", 2)
    a1, b1 = attend(chunk_rows, chunk_rows, qkv, row_owner[chunk_rows:, None], row_owner[None, :])
    xa0, yb0, a1, b1, ya, xb = stage(xa0, yb0, a1, b1, ya, xb)

    a0, b0 = jnp.stack([a0, xa0]), jnp.stack([b0, yb0])
    ya0, xb0 = swap(a0, "blk", 2), swap(b0, "blk", 1)
    xa1, yb1 = swap(a1, "blk", 1), swap(b1, "blk", 2)
    wo_own = jnp.concatenate([a, ya, b, xb], axis=0)
    wos = [wo_own, swap(wo_own, "tok", 1)]
    a0, ya0, b0, xb0, xa1, yb1, *wos = stage(a0, ya0, b0, xb0, xa1, yb1, *wos)
    a1, b1 = jnp.stack([a1, xa1]), jnp.stack([b1, yb1])
    ya1, xb1 = swap(a1, "blk", 2), swap(b1, "blk", 1)

    def dense(atts, n):
        return mlp(
            n * chunk_rows, chunk_rows, where, slots, atts, wos, moved, out_bias[None, :],
            ln2_gain[None, :], ln2_bias[None, :], w_fc1, fc1_bias[None, :], w_fc2, fc2_bias[None, :],
        )

    own0, *sends0 = dense([a0, ya0, b0, xb0], 0)
    own0, *sends0, a1, ya1, b1, xb1 = stage(own0, *sends0, a1, ya1, b1, xb1)
    parts0 = [swap(x, "blk", r) for r, x in enumerate(sends0, 1)]
    own1, *sends1 = dense([a1, ya1, b1, xb1], 1)
    own1, *rest = stage(own1, *sends1, *parts0)
    sends1, parts0 = rest[:3], rest[3:]
    parts1 = [swap(x, "blk", r) for r, x in enumerate(sends1, 1)]

    gain3 = lax.dynamic_slice_in_dim(ln3_gain, blk * quarter, quarter, 0)
    bias3 = lax.dynamic_slice_in_dim(ln3_bias, blk * quarter, quarter, 0)
    if split_proj:
        *parts1, proj_own = stage(*parts1, proj_own)
    else:
        parts1 = stage(*parts1)
    own = jnp.concatenate([own0, own1], axis=1)
    for x0, x1 in zip(parts0, parts1):
        own = own + jnp.concatenate([x0, x1], axis=1).astype(F32)
    layer = own.astype(BF16)
    wide = layer.astype(F32)
    mean = jnp.mean(wide, axis=0)
    centered = wide - mean[None, :]
    spread = jnp.sum(centered * centered, axis=0)
    if split_proj:
        proj_own, mean, spread = stage(proj_own, mean, spread)
        proj_other = swap(proj_own, "tok", 1)
    seen = quarter
    for r in (1, 2):
        other = swap(jnp.stack([mean, spread]), "blk", r)
        spread = spread + other[1] + (mean - other[0]) ** 2 * (seen / 2)
        mean = (mean + other[0]) * 0.5
        seen *= 2
    stats = jnp.stack([lax.rsqrt(spread / width + EPS), mean])
    own, *sends = project(where, layer, stats, gain3[:, None], bias3[:, None], proj_own, proj_other)
    for r, x in enumerate(sends, 1):
        own = own + swap(x, "blk", r).astype(F32)
    projected = (own + proj_bias[:, None]).astype(BF16)

    slot_cap = 2 * merged_count // tok_count
    first = jnp.sum((owner_sorted[None, :] < owner_sorted[:, None]).astype(jnp.int32), axis=1)
    target = owner_sorted * slot_cap + order - first
    placed = (jnp.arange(tok_count * slot_cap, dtype=jnp.int32)[:, None] == target[None, :]).astype(BF16)
    outgoing = lax.dot_general(placed, projected, (((1,), (1,)), ((), ())), preferred_element_type=F32).astype(BF16)
    outgoing = outgoing.reshape(tok_count, slot_cap, quarter)
    arrived = lax.all_to_all(outgoing, "tok", split_axis=0, concat_axis=0, tiled=True)
    return arrived[None]


def solution(mesh):
    placed = (
        P("tok", "blk", None),
        P("tok", None),
        P("tok", None, None),
        P("tok", None),
        P(),
        P(),
        P(None, "tok", "blk"),
        P(None, "blk"),
        P("blk", "tok"),
        P(),
        P(),
        P(),
        P(None, "blk"),
        P("blk"),
        P("blk", None),
        P(),
        P(),
        P(),
        P("tok", "blk"),
        P("blk"),
    )
    return jax.shard_map(
        body, mesh=mesh, in_specs=placed, out_specs=P("tok", None, None, "blk"), check_vma=False
    )
```

```python
import functools
import math

import jax
import jax.numpy as jnp
from jax import lax
from jax.experimental import pallas as pl
from jax.experimental.pallas import tpu as pltpu
from jax.sharding import PartitionSpec as P

HD = 104
EPS = 1e-06
CHUNKS = 2
BF16 = jnp.bfloat16
F32 = jnp.float32
VM = pl.BlockSpec(memory_space=pltpu.VMEM)
SM = pl.BlockSpec(memory_space=pltpu.SMEM)
ANY = pl.BlockSpec(memory_space=pl.ANY)


def cost(flops, nbytes, trans=0):
    return pl.CostEstimate(flops=int(flops), bytes_accessed=int(nbytes), transcendentals=int(trans))


def params(mib):
    return pltpu.CompilerParams(vmem_limit_bytes=mib * 1024 * 1024)


def norm(x, gain, bias):
    center = x - jnp.mean(x, axis=-1, keepdims=True)
    spread = jnp.mean(center * center, axis=-1, keepdims=True)
    return center * lax.rsqrt(spread + EPS) * gain + bias


def swap(x, axis, mask):
    return lax.ppermute(x, axis, [(i, i ^ mask) for i in range(lax.axis_size(axis))])


def stage(*arrays):
    return lax.optimization_barrier(arrays)


def same_core_groups(count):
    return [list(range(core, count, 2)) for core in range(2)]


def permute_norm_kernel(count, perm, place, gain, bias, *refs):
    pieces, (moved, normed, tok, sems) = refs[:count], refs[count:]

    @pl.when(pl.program_id(0) == 0)
    def _():
        copies, start = [], 0
        for n, piece in enumerate(pieces):
            size = piece.shape[0]
            copies.append(pltpu.make_async_copy(piece, tok.at[pl.ds(start, size), :], sems.at[n]))
            start += size
        for copy in copies:
            copy.start()
        for copy in copies:
            copy.wait()

    pick = (perm[...] == place[...]).astype(F32).astype(BF16)
    rows = jnp.dot(pick, tok[...], preferred_element_type=F32)
    moved[...] = rows.astype(BF16)
    normed[...] = norm(rows, gain[...], bias[...]).astype(BF16)


def permute_norm(perm, place, pieces, gain, bias):
    rows, width = perm.shape[0], pieces[0].shape[1]
    step = 256
    return pl.pallas_call(
        functools.partial(permute_norm_kernel, len(pieces)),
        grid=(rows // step,),
        in_specs=[
            pl.BlockSpec((step, 1), lambda i: (i, 0)),
            pl.BlockSpec((1, rows), lambda i: (0, 0)),
            pl.BlockSpec((1, width), lambda i: (0, 0)),
            pl.BlockSpec((1, width), lambda i: (0, 0)),
        ]
        + [ANY] * len(pieces),
        out_specs=[pl.BlockSpec((step, width), lambda i: (i, 0))] * 2,
        out_shape=[jax.ShapeDtypeStruct((rows, width), BF16)] * 2,
        scratch_shapes=[pltpu.VMEM((rows, width), BF16), pltpu.SemaphoreType.DMA((len(pieces),))],
        compiler_params=params(56),
        cost_estimate=cost(2 * rows * rows * width, 6 * rows * width),
        name="permute_norm",
    )(perm, place, gain, bias, *pieces)


def transpose_kernel(x, out):
    out[...] = x[...].T


def transpose(x):
    return pl.pallas_call(
        transpose_kernel,
        in_specs=[VM],
        out_specs=VM,
        out_shape=jax.ShapeDtypeStruct(x.shape[::-1], x.dtype),
        compiler_params=params(8),
        cost_estimate=cost(0, 4 * x.size),
        name="transpose",
    )(x)


def qkv_kernel(core, h, own, other, bias, out, weight, sems):
    groups, _, shard, _ = own.shape
    me = core[0]
    copies = []
    for z in range(groups):
        for n, (src, c) in enumerate(((own, me), (other, 1 - me))):
            start = pl.multiple_of((2 * z + c) * shard, 16)
            copy = pltpu.make_async_copy(src.at[z], weight.at[:, pl.ds(start, shard), :], sems.at[n, z])
            copy.start()
            copies.append(copy)
    for copy in copies:
        copy.wait()
    rows = h.shape[0]
    step = 256

    for part in range(3):

        @pl.loop(0, rows // step)
        def _(i):
            at = pl.ds(pl.multiple_of(i * step, step), step)
            acc = jnp.dot(h[at, :], weight[part], preferred_element_type=F32)
            out[part, at, :] = (acc + bias[part : part + 1, :]).astype(BF16)


def qkv_project(core, h, own, other, bias):
    groups, parts, shard, cols = own.shape
    rows, width = h.shape
    return pl.pallas_call(
        qkv_kernel,
        in_specs=[SM, VM, ANY, ANY, VM],
        out_specs=VM,
        out_shape=jax.ShapeDtypeStruct((parts, rows, cols), BF16),
        scratch_shapes=[
            pltpu.VMEM((parts, width, cols), BF16),
            pltpu.SemaphoreType.DMA((2, groups)),
        ],
        compiler_params=params(24),
        cost_estimate=cost(2 * rows * width * parts * cols, 12e6),
        name="qkv_project",
    )(core, h, own, other, bias)


def attend_kernel(first, qkv, row_owner, col_owner, *outs):
    cols, step = outs[0].shape
    scale = math.log2(math.e) / math.sqrt(HD)
    keys = qkv.shape[1]
    for head in range(cols // HD):
        at = slice(head * HD, head * HD + HD)
        key = qkv[1, :, at]
        value = jnp.concatenate([qkv[2, :, at], jnp.ones((keys, 128 - HD), BF16)], axis=1)
        for n, out in enumerate(outs):
            start = n * step
            mine = slice(start, start + step)
            query = qkv[0, first + start : first + start + step, at]
            scores = lax.dot_general(query, key, (((1,), (1,)), ((), ())), preferred_element_type=F32)
            kept = row_owner[mine, :] == col_owner[...]
            weights = jnp.where(kept, jnp.exp2(scores * scale), 0.0).astype(BF16)
            mixed = jnp.dot(weights, value, preferred_element_type=F32)
            out[at, :] = (mixed / mixed[:, HD : HD + 1]).T[:HD, :].astype(BF16)


def attend(first, rows, qkv, row_owner, col_owner):
    _, keys, cols = qkv.shape
    return pl.pallas_call(
        functools.partial(attend_kernel, first),
        in_specs=[VM] * 3,
        out_specs=[VM] * 2,
        out_shape=[jax.ShapeDtypeStruct((cols, rows // 2), BF16)] * 2,
        compiler_params=params(16),
        cost_estimate=cost(4 * rows * keys * cols, 4e6, rows * keys * (cols // HD)),
        name="attend",
    )(qkv, row_owner, col_owner)


def mlp_kernel(first, where, out_bias, gain, bias, b1, b2, tok, w1, w2, *refs):
    atts, wos, (mine, to1, to2, to3, *scratch) = refs[:4], refs[4:12], refs[12:]
    tok_in, att_in, w1_in, w2_in, wo, total, h, hidden, sem_a, sem_o, sem_w = scratch
    core, me = where[0], where[1]
    quarter, rows = mine.shape
    step = rows // 2
    early = [pltpu.make_async_copy(tok.at[first : first + rows, :], tok_in, sem_a.at[4])]
    for n, src in enumerate(atts):
        early.append(pltpu.make_async_copy(src, att_in.at[n], sem_a.at[n]))
    count, slots = wos[0].shape[1], sem_o.shape[2]
    size = min(count, wo.shape[1] // 2 // slots)
    for n in range(2):
        for m, r in enumerate((0, 1, 2, 3, 0, 2, 1, 3)):
            for p in range(count // size):
                row = (m // 4) * count + p * size
                slot, off = divmod(row, wo.shape[1] // 2 // slots)
                place = (where[2] ^ (2 * slot) ^ n) * (wo.shape[1] // 2 // slots) + off
                start = pl.multiple_of(place, 16)
                early.append(
                    pltpu.make_async_copy(
                        wos[4 * n + m // 2].at[m % 2, p * size : p * size + size, :],
                        wo.at[r, pl.ds(start, size), :],
                        sem_o.at[n, m, p],
                    )
                )
    parts = sem_w.shape[1]
    late = []
    for n, (src, dst) in enumerate(((w1, w1_in), (w2, w2_in))):
        size = src.shape[0] // parts
        cuts = [slice(p * size, p * size + size) for p in range(parts)]
        late.append(
            [pltpu.make_async_copy(src.at[at, :], dst.at[at, :], sem_w.at[n, p]) for p, at in enumerate(cuts)]
        )
    for copy in early:
        copy.start()
    for copy in early:
        copy.wait()
    for copy in late[0] + late[1]:
        copy.start()

    for n, pairs in enumerate((((0, (0, 1)), (1, (2, 3))), ((2, (0, 2)), (3, (1, 3))))):
        at = slice(n * step, n * step + step)
        summed = tok_in[at, :].astype(F32) + out_bias[...]
        for a, places in pairs:
            for m, r in enumerate(places):
                summed = summed + lax.dot_general(
                    att_in[a, m],
                    wo[r],
                    (((0,), (1,)), ((), ())),
                    preferred_element_type=F32,
                )
        total[at, :] = summed
        h[at, :] = norm(summed, gain[...], bias[...]).astype(BF16)

    for copy in late[0]:
        copy.wait()
    tile = 512

    @pl.loop(0, rows // step)
    def _(i):
        at = pl.ds(pl.multiple_of(i * step, step), step)
        for start in range(0, w1.shape[1], tile):
            cols = slice(start, start + tile)
            pre = jnp.dot(h[at, :], w1_in[:, cols], preferred_element_type=F32) + b1[:, cols]
            hidden[at, cols] = (0.5 * pre * (1.0 + lax.erf(pre * math.sqrt(0.5)))).astype(BF16)

    for place in range(4):

        @pl.when(me == place)
        def _(place=place):
            at = slice(place * quarter, place * quarter + quarter)
            mine[...] = (total[:, at] + b2[:, at]).T

    for copy in late[1]:
        copy.wait()

    @pl.loop(0, rows // step)
    def _(i):
        at = pl.ds(pl.multiple_of(i * step, step), step)
        total[at, :] = jnp.dot(hidden[at, :], w2_in[...], preferred_element_type=F32)

    for place in range(4):

        @pl.when(me == place)
        def _(place=place):
            mine[...] += total[:, place * quarter : place * quarter + quarter].T
            for r, ref in ((1, to1), (2, to2), (3, to3)):
                start = (place ^ r) * quarter
                ref[...] = total[:, start : start + quarter].T.astype(BF16)


def mlp(first, rows, where, slots, atts, wos, tok, out_bias, gain, bias, w1, b1, w2, b2):
    width = tok.shape[1]
    hidden = w1.shape[1]
    quarter = width // 4
    parts = 4
    return pl.pallas_call(
        functools.partial(mlp_kernel, first),
        in_specs=[SM] + [VM] * 5 + [ANY] * (3 + len(atts) + len(wos)),
        out_specs=[VM] * 4,
        out_shape=[jax.ShapeDtypeStruct((quarter, rows), F32)]
        + [jax.ShapeDtypeStruct((quarter, rows), BF16)] * 3,
        scratch_shapes=[
            pltpu.VMEM((rows, width), BF16),
            pltpu.VMEM((len(atts), *atts[0].shape), BF16),
            pltpu.VMEM(w1.shape, BF16),
            pltpu.VMEM(w2.shape, BF16),
            pltpu.VMEM((4, width, quarter), BF16),
            pltpu.VMEM((rows, width), F32),
            pltpu.VMEM((rows, width), BF16),
            pltpu.VMEM((rows, hidden), BF16),
            pltpu.SemaphoreType.DMA((len(atts) + 1,)),
            pltpu.SemaphoreType.DMA((2, 8, slots)),
            pltpu.SemaphoreType.DMA((2, parts)),
        ],
        compiler_params=params(52),
        cost_estimate=cost(2 * rows * width * (width + 2 * hidden), 25e6, rows * hidden),
        name="out_mlp",
    )(where, out_bias, gain, bias, b1, b2, tok, w1, w2, *atts, *wos)


def hold_kernel(where, own, other, wp, sems):
    folds, shard, _ = own.shape
    copies = []
    for k in range(folds):
        for n, src in enumerate((own, other)):
            start = pl.multiple_of((2 * k + (where[0] ^ n)) * shard, 16)
            copies.append(pltpu.make_async_copy(src.at[k], wp.at[pl.ds(start, shard), :], sems.at[n, k]))
    for copy in copies:
        copy.start()
    for copy in copies:
        copy.wait()


def hold(where, own, other):
    folds, shard, width = own.shape
    return pl.pallas_call(
        hold_kernel,
        in_specs=[SM, ANY, ANY],
        out_specs=VM,
        out_shape=jax.ShapeDtypeStruct((2 * folds * shard, width), BF16),
        scratch_shapes=[pltpu.SemaphoreType.DMA((2, folds))],
        compiler_params=params(48),
        cost_estimate=cost(0, 11e6),
        name="hold",
    )(where, own, other)


def project_kernel(folds, where, layer, stats, gain, bias, wp, mine, to1, to2, to3, acc):
    me = where[1]
    quarter = mine.shape[0]
    scale, shift = stats[0:1, :], stats[1:2, :]
    final = ((layer[...].astype(F32) - shift) * scale * gain[...] + bias[...]).astype(BF16)
    depth = wp.shape[0] // folds
    each = final.shape[1] // folds // CHUNKS
    for n in range(CHUNKS):
        part = 0.0
        for k in range(folds):
            start = (n * folds + k) * each
            part = part + lax.dot_general(
                final[:, start : start + each],
                wp[k * depth : k * depth + depth, :],
                (((0,), (0,)), ((), ())),
                preferred_element_type=F32,
            )
        acc[n * each : n * each + each, :] = part
    for place in range(4):

        @pl.when(me == place)
        def _(place=place):
            at = slice(place * quarter, place * quarter + quarter)
            mine[...] = acc[:, at].T
            for r, ref in ((1, to1), (2, to2), (3, to3)):
                first = (place ^ r) * quarter
                ref[...] = acc[:, first : first + quarter].T.astype(BF16)


def project(folds, where, layer, stats, gain, bias, wp):
    width = wp.shape[1]
    count = layer.shape[1] // folds
    quarter = width // 4
    return pl.pallas_call(
        functools.partial(project_kernel, folds),
        in_specs=[SM] + [VM] * 5,
        out_specs=[VM] * 4,
        out_shape=[jax.ShapeDtypeStruct((quarter, count), F32)]
        + [jax.ShapeDtypeStruct((quarter, count), BF16)] * 3,
        scratch_shapes=[pltpu.VMEM((count, width), F32)],
        compiler_params=params(16),
        cost_estimate=cost(2 * count * wp.size, 7e6),
        name="project",
    )(where, layer, stats, gain, bias, wp)


def gather_qkv(w_qkv, core):
    parts, shard, cols = w_qkv.shape
    count = lax.axis_size("tok")
    if shard % 16:
        whole = lax.all_gather(w_qkv, "tok", axis=1, tiled=True)
        low, high = whole[None, :, : whole.shape[1] // 2], whole[None, :, whole.shape[1] // 2 :]
        return jnp.where(core == 0, low, high), jnp.where(core == 0, high, low)
    own = lax.all_gather(
        w_qkv.reshape(parts * shard, cols), "tok", axis=0, tiled=True, axis_index_groups=same_core_groups(count)
    ).reshape(count // 2, parts, shard, cols)
    return own, None


def gather_proj_whole(w_proj, core):
    _, quarter = w_proj.shape
    whole = lax.all_gather(w_proj, "tok", axis=0, tiled=True).reshape(4, 4, quarter, quarter)
    whole = lax.all_to_all(whole, "blk", split_axis=1, concat_axis=3, tiled=True)
    whole = whole.reshape(4, 2, quarter // 2, 4 * quarter)
    low, high = whole[:, 0], whole[:, 1]
    return jnp.where(core == 0, low, high), jnp.where(core == 0, high, low)


def body(
    tokens,
    segment_ids,
    merge_index,
    segment_owner,
    ln1_gain,
    ln1_bias,
    w_qkv,
    qkv_bias,
    w_out,
    out_bias,
    ln2_gain,
    ln2_bias,
    w_fc1,
    fc1_bias,
    w_fc2,
    fc2_bias,
    ln3_gain,
    ln3_bias,
    w_proj,
    proj_bias,
):
    blk, tok = lax.axis_index("blk"), lax.axis_index("tok")
    core = tok % 2
    tok_count = lax.axis_size("tok")
    block = tokens[0]
    local_rows, width = block.shape
    rows = 4 * local_rows
    quarter = width // 4
    merges = merge_index[0]
    merged_count, folds = merges.shape

    half = local_rows // 2
    split_proj = w_proj.shape[0] == 2 * quarter and tok_count == 8
    even, low = (blk & 1) == 0, (blk & 2) == 0

    qkv_own, qkv_other = gather_qkv(w_qkv, core)
    a, b = block[:half], block[half:]
    depth, shard = w_out.shape
    if shard % 16:
        whole = lax.all_gather(w_out, "tok", axis=1, tiled=True).T
        shards = [lax.dynamic_slice_in_dim(whole, core * (width // 2), width // 2, 0)]
        where = jnp.stack([core, blk, core]).astype(jnp.int32)
    else:
        shards = [transpose(w_out)]
        shards += [swap(shards[0], "tok", 2 * n) for n in range(1, tok_count // 2)]
        where = jnp.stack([core, blk, tok]).astype(jnp.int32)
    xa, yb = swap(a, "blk", 1), swap(b, "blk", 2)
    xa, yb = stage(xa, yb)

    a, b = jnp.concatenate([a, xa], axis=0), jnp.concatenate([b, yb], axis=0)
    ya, xb = swap(a, "blk", 2), swap(b, "blk", 1)
    if split_proj:
        halves = stage(w_proj, a)[0].reshape(2, 2, quarter // 2, quarter)
        keep = jnp.where(core == 0, halves[:, 0], halves[:, 1])
        got = swap(jnp.where(core == 0, halves[:, 1], halves[:, 0]), "tok", 1)
        near = jnp.where((core == 0) == low, keep, got)
        far = jnp.where((core == 0) == low, got, keep)
        ya, xb, near, far = stage(ya, xb, near, far)
    else:
        ya, xb = stage(ya, xb)
    pieces = [a, ya, b, xb]

    ids = jnp.arange(rows, dtype=jnp.int32)
    seg_of = jnp.sum(jnp.where(merges[:, :1] == ids[None, :], segment_ids[0][None, :], 0), axis=1)
    owners = segment_owner[0]
    owner = jnp.sum(
        jnp.where(seg_of[:, None] == jnp.arange(owners.shape[0], dtype=jnp.int32)[None, :], owners[None, :], 0),
        axis=1,
    )
    order = jnp.arange(merged_count, dtype=jnp.int32)
    ahead = (owner[None, :] < owner[:, None]) | ((owner[None, :] == owner[:, None]) & (order[None, :] < order[:, None]))
    place = jnp.sum(ahead.astype(jnp.int32), axis=1)
    at_place = place[None, :] == order[:, None]
    owner_sorted = jnp.sum(jnp.where(at_place, owner[None, :], 0), axis=1)
    merges_sorted = jnp.sum(jnp.where(at_place[:, :, None], merges[None, :, :], 0), axis=1)
    chunks = CHUNKS
    count = merged_count // chunks
    perm = merges_sorted.reshape(chunks, count, folds).transpose(0, 2, 1).reshape(rows, 1)
    row_owner = jnp.broadcast_to(owner_sorted.reshape(chunks, 1, count), (chunks, folds, count)).reshape(rows)
    nth = ids // half
    swapped = (nth & 1) * 2 + (nth & 2) // 2
    device = jnp.where(nth < 4, nth, swapped) ^ blk
    source = device * local_rows + jnp.where(nth < 4, 0, half) + ids % half

    if split_proj:
        got, ya, xb = stage(swap(far, "blk", 2), ya, xb)
        pair = jnp.concatenate([jnp.where(low, near, got), jnp.where(low, got, near)], axis=2)
        keep, give = jnp.where(even, pair[0], pair[1]), jnp.where(even, pair[1], pair[0])
        pieces = [a, ya, b, xb]

    moved, normed = permute_norm(perm, source[None, :], pieces, ln1_gain[None, :], ln1_bias[None, :])
    if split_proj:
        got, moved, normed, *shards = stage(swap(give, "blk", 1), moved, normed, *shards)
    else:
        moved, normed, *shards = stage(moved, normed, *shards)

    slots = len(shards)
    shards = jnp.concatenate(shards, axis=0)
    a, b = shards[: width // 4], shards[width // 4 :]
    xa, yb = swap(a, "blk", 1), swap(b, "blk", 2)
    if split_proj:
        one, two = jnp.where(even, keep, got), jnp.where(even, got, keep)
        mine = jnp.concatenate([one[:, :quarter], two[:, :quarter], one[:, quarter:], two[:, quarter:]], axis=1)
        xa, yb, qkv_own, mine = stage(xa, yb, qkv_own, mine)
        proj_own = lax.all_gather(mine, "tok", axis=0, tiled=True, axis_index_groups=same_core_groups(tok_count))
        proj_own = proj_own.reshape(4, quarter // 2, width)
    else:
        xa, yb, qkv_own = stage(xa, yb, qkv_own)
        proj_own, proj_other = gather_proj_whole(w_proj, core)

    a, b = jnp.stack([a, xa]), jnp.stack([b, yb])
    ya, xb = swap(a, "blk", 2), swap(b, "blk", 1)
    if qkv_other is None:
        qkv_other = swap(qkv_own, "tok", 1)
    qkv = qkv_project(where, normed, qkv_own, qkv_other, qkv_bias)
    qkv, ya, xb = stage(qkv, ya, xb)

    chunk_rows = rows // chunks
    wos = [a, ya, b, xb]
    wos += [swap(x, "tok", 1) for x in wos]
    a0, b0 = attend(0, chunk_rows, qkv, row_owner[:chunk_rows, None], row_owner[None, :])
    a0, b0, qkv, *wos = stage(a0, b0, qkv, *wos)

    xa0, yb0 = swap(a0, "blk", 1), swap(b0, "blk", 2)
    a1, b1 = attend(chunk_rows, chunk_rows, qkv, row_owner[chunk_rows:, None], row_owner[None, :])
    xa0, yb0, a1, b1 = stage(xa0, yb0, a1, b1)

    a0, b0 = jnp.stack([a0, xa0]), jnp.stack([b0, yb0])
    ya0, xb0 = swap(a0, "blk", 2), swap(b0, "blk", 1)
    xa1, yb1 = swap(a1, "blk", 1), swap(b1, "blk", 2)
    gain3 = lax.dynamic_slice_in_dim(ln3_gain, blk * quarter, quarter, 0)
    bias3 = lax.dynamic_slice_in_dim(ln3_bias, blk * quarter, quarter, 0)
    a0, ya0, b0, xb0, xa1, yb1, gain3, bias3 = stage(a0, ya0, b0, xb0, xa1, yb1, gain3, bias3)
    a1, b1 = jnp.stack([a1, xa1]), jnp.stack([b1, yb1])
    ya1, xb1 = swap(a1, "blk", 2), swap(b1, "blk", 1)

    def dense(atts, n):
        return mlp(
            n * chunk_rows, chunk_rows, where, slots, atts, wos, moved, out_bias[None, :],
            ln2_gain[None, :], ln2_bias[None, :], w_fc1, fc1_bias[None, :], w_fc2, fc2_bias[None, :],
        )

    own0, *sends0 = dense([a0, ya0, b0, xb0], 0)
    own0, *sends0, a1, ya1, b1, xb1 = stage(own0, *sends0, a1, ya1, b1, xb1)
    if split_proj:
        proj_own, own0 = stage(proj_own, own0)
        proj_other = swap(proj_own, "tok", 1)
    parts0 = [swap(x, "blk", r) for r, x in enumerate(sends0, 1)]
    own1, *sends1 = dense([a1, ya1, b1, xb1], 1)
    own1, proj_other, *rest = stage(own1, proj_other, *sends1, *parts0)
    sends1, parts0 = rest[:3], rest[3:]
    parts1 = [swap(x, "blk", r) for r, x in enumerate(sends1, 1)]

    wp = hold(where, proj_own, proj_other)
    *parts1, wp = stage(*parts1, wp)
    own = jnp.concatenate([own0, own1], axis=1)
    for x0, x1 in zip(parts0, parts1):
        own = own + jnp.concatenate([x0, x1], axis=1).astype(F32)
    layer = own.astype(BF16)
    wide = layer.astype(F32)
    mean = jnp.mean(wide, axis=0)
    centered = wide - mean[None, :]
    spread = jnp.sum(centered * centered, axis=0)
    seen = quarter
    for r in (1, 2):
        other = swap(jnp.stack([mean, spread]), "blk", r)
        spread = spread + other[1] + (mean - other[0]) ** 2 * (seen / 2)
        mean = (mean + other[0]) * 0.5
        seen *= 2
    stats = jnp.stack([lax.rsqrt(spread / width + EPS), mean])
    own, *sends = project(folds, where, layer, stats, gain3[:, None], bias3[:, None], wp)
    for r, x in enumerate(sends, 1):
        own = own + swap(x, "blk", r).astype(F32)
    projected = (own + proj_bias[:, None]).astype(BF16)

    slot_cap = 2 * merged_count // tok_count
    first = jnp.sum((owner_sorted[None, :] < owner_sorted[:, None]).astype(jnp.int32), axis=1)
    target = owner_sorted * slot_cap + order - first
    placed = (jnp.arange(tok_count * slot_cap, dtype=jnp.int32)[:, None] == target[None, :]).astype(BF16)
    outgoing = lax.dot_general(placed, projected, (((1,), (1,)), ((), ())), preferred_element_type=F32).astype(BF16)
    outgoing = outgoing.reshape(tok_count, slot_cap, quarter)
    arrived = lax.all_to_all(outgoing, "tok", split_axis=0, concat_axis=0, tiled=True)
    return arrived[None]


def solution(mesh):
    placed = (
        P("tok", "blk", None),
        P("tok", None),
        P("tok", None, None),
        P("tok", None),
        P(),
        P(),
        P(None, "tok", "blk"),
        P(None, "blk"),
        P("blk", "tok"),
        P(),
        P(),
        P(),
        P(None, "blk"),
        P("blk"),
        P("blk", None),
        P(),
        P(),
        P(),
        P("tok", "blk"),
        P("blk"),
    )
    return jax.shard_map(
        body, mesh=mesh, in_specs=placed, out_specs=P("tok", None, None, "blk"), check_vma=False
    )
```

```python
import functools
import math

import jax
import jax.numpy as jnp
from jax import lax
from jax.experimental import pallas as pl
from jax.experimental.pallas import tpu as pltpu
from jax.sharding import PartitionSpec as P

HD = 104
EPS = 1e-06
CHUNKS = 2
BF16 = jnp.bfloat16
F32 = jnp.float32
VM = pl.BlockSpec(memory_space=pltpu.VMEM)
SM = pl.BlockSpec(memory_space=pltpu.SMEM)
ANY = pl.BlockSpec(memory_space=pl.ANY)


def cost(flops, nbytes, trans=0):
    return pl.CostEstimate(flops=int(flops), bytes_accessed=int(nbytes), transcendentals=int(trans))


def params(mib):
    return pltpu.CompilerParams(vmem_limit_bytes=mib * 1024 * 1024)


def norm(x, gain, bias):
    center = x - jnp.mean(x, axis=-1, keepdims=True)
    spread = jnp.mean(center * center, axis=-1, keepdims=True)
    return center * lax.rsqrt(spread + EPS) * gain + bias


def swap(x, axis, mask):
    return lax.ppermute(x, axis, [(i, i ^ mask) for i in range(lax.axis_size(axis))])


def stage(*arrays):
    return lax.optimization_barrier(arrays)


def same_core_groups(count):
    return [list(range(core, count, 2)) for core in range(2)]


def permute_norm_kernel(count, perm, place, gain, bias, *refs):
    pieces, (moved, normed, tok, sems) = refs[:count], refs[count:]

    @pl.when(pl.program_id(0) == 0)
    def _():
        copies, start = [], 0
        for n, piece in enumerate(pieces):
            size = piece.shape[0]
            copies.append(pltpu.make_async_copy(piece, tok.at[pl.ds(start, size), :], sems.at[n]))
            start += size
        for copy in copies:
            copy.start()
        for copy in copies:
            copy.wait()

    pick = (perm[...] == place[...]).astype(F32).astype(BF16)
    rows = jnp.dot(pick, tok[...], preferred_element_type=F32)
    moved[...] = rows.astype(BF16)
    normed[...] = norm(rows, gain[...], bias[...]).astype(BF16)


def permute_norm(perm, place, pieces, gain, bias):
    rows, width = perm.shape[0], pieces[0].shape[1]
    step = 256
    return pl.pallas_call(
        functools.partial(permute_norm_kernel, len(pieces)),
        grid=(rows // step,),
        in_specs=[
            pl.BlockSpec((step, 1), lambda i: (i, 0)),
            pl.BlockSpec((1, rows), lambda i: (0, 0)),
            pl.BlockSpec((1, width), lambda i: (0, 0)),
            pl.BlockSpec((1, width), lambda i: (0, 0)),
        ]
        + [ANY] * len(pieces),
        out_specs=[pl.BlockSpec((step, width), lambda i: (i, 0))] * 2,
        out_shape=[jax.ShapeDtypeStruct((rows, width), BF16)] * 2,
        scratch_shapes=[pltpu.VMEM((rows, width), BF16), pltpu.SemaphoreType.DMA((len(pieces),))],
        compiler_params=params(56),
        cost_estimate=cost(2 * rows * rows * width, 6 * rows * width),
        name="permute_norm",
    )(perm, place, gain, bias, *pieces)


def transpose_kernel(x, out):
    out[...] = x[...].T


def transpose(x):
    return pl.pallas_call(
        transpose_kernel,
        in_specs=[VM],
        out_specs=VM,
        out_shape=jax.ShapeDtypeStruct(x.shape[::-1], x.dtype),
        compiler_params=params(8),
        cost_estimate=cost(0, 4 * x.size),
        name="transpose",
    )(x)


def attend_rows(first, qkv, row_owner, col_owner, *outs):
    cols, step = outs[0].shape
    scale = math.log2(math.e) / math.sqrt(HD)
    keys = qkv.shape[1]
    for head in range(cols // HD):
        at = slice(head * HD, head * HD + HD)
        key = qkv[1, :, at]
        value = jnp.concatenate([qkv[2, :, at], jnp.ones((keys, 128 - HD), BF16)], axis=1)
        for n, out in enumerate(outs):
            start = n * step
            mine = slice(start, start + step)
            query = qkv[0, first + start : first + start + step, at]
            scores = lax.dot_general(query, key, (((1,), (1,)), ((), ())), preferred_element_type=F32)
            kept = row_owner[mine, :] == col_owner[...]
            weights = jnp.where(kept, jnp.exp2(scores * scale), 0.0).astype(BF16)
            mixed = jnp.dot(weights, value, preferred_element_type=F32)
            out[at, :] = (mixed / mixed[:, HD : HD + 1]).T[:HD, :].astype(BF16)


def qkv_attend_kernel(core, h, own, other, bias, row_owner, col_owner, *refs):
    *outs, out, weight, sems = refs
    groups, _, shard, _ = own.shape
    me = core[0]
    copies = []
    for z in range(groups):
        for n, (src, c) in enumerate(((own, me), (other, 1 - me))):
            start = pl.multiple_of((2 * z + c) * shard, 16)
            copy = pltpu.make_async_copy(src.at[z], weight.at[:, pl.ds(start, shard), :], sems.at[n, z])
            copy.start()
            copies.append(copy)
    for copy in copies:
        copy.wait()
    rows = h.shape[0]
    step = 256

    for part in range(3):

        @pl.loop(0, rows // step)
        def _(i):
            at = pl.ds(pl.multiple_of(i * step, step), step)
            acc = jnp.dot(h[at, :], weight[part], preferred_element_type=F32)
            out[part, at, :] = (acc + bias[part : part + 1, :]).astype(BF16)

    chunk = rows // CHUNKS
    for n in range(CHUNKS):
        attend_rows(n * chunk, out, row_owner.at[n * chunk : n * chunk + chunk, :], col_owner, *outs[2 * n : 2 * n + 2])


def qkv_attend(core, h, own, other, bias, row_owner, col_owner):
    groups, parts, shard, cols = own.shape
    rows, width = h.shape
    return pl.pallas_call(
        qkv_attend_kernel,
        in_specs=[SM, VM, ANY, ANY, VM, VM, VM],
        out_specs=[VM] * (2 * CHUNKS),
        out_shape=[jax.ShapeDtypeStruct((cols, rows // CHUNKS // 2), BF16)] * (2 * CHUNKS),
        scratch_shapes=[
            pltpu.VMEM((parts, rows, cols), BF16),
            pltpu.VMEM((parts, width, cols), BF16),
            pltpu.SemaphoreType.DMA((2, groups)),
        ],
        compiler_params=params(32),
        cost_estimate=cost(2 * rows * width * parts * cols + 4 * rows * rows * cols, 16e6, rows * rows * (cols // HD)),
        name="qkv_attend",
    )(core, h, own, other, bias, row_owner, col_owner)


def mlp_kernel(first, where, out_bias, gain, bias, b1, b2, tok, w1, w2, *refs):
    atts, wos, (mine, to1, to2, to3, *scratch) = refs[:4], refs[4:12], refs[12:]
    tok_in, att_in, w1_in, w2_in, wo, total, h, hidden, sem_a, sem_o, sem_w = scratch
    core, me = where[0], where[1]
    quarter, rows = mine.shape
    step = rows // 2
    early = [pltpu.make_async_copy(tok.at[first : first + rows, :], tok_in, sem_a.at[4])]
    for n, src in enumerate(atts):
        early.append(pltpu.make_async_copy(src, att_in.at[n], sem_a.at[n]))
    count, slots = wos[0].shape[1], sem_o.shape[2]
    size = min(count, wo.shape[1] // 2 // slots)
    for n in range(2):
        for m, r in enumerate((0, 1, 2, 3, 0, 2, 1, 3)):
            for p in range(count // size):
                row = (m // 4) * count + p * size
                slot, off = divmod(row, wo.shape[1] // 2 // slots)
                place = (where[2] ^ (2 * slot) ^ n) * (wo.shape[1] // 2 // slots) + off
                start = pl.multiple_of(place, 16)
                early.append(
                    pltpu.make_async_copy(
                        wos[4 * n + m // 2].at[m % 2, p * size : p * size + size, :],
                        wo.at[r, pl.ds(start, size), :],
                        sem_o.at[n, m, p],
                    )
                )
    parts = sem_w.shape[1]
    late = []
    for n, (src, dst) in enumerate(((w1, w1_in), (w2, w2_in))):
        size = src.shape[0] // parts
        cuts = [slice(p * size, p * size + size) for p in range(parts)]
        late.append(
            [pltpu.make_async_copy(src.at[at, :], dst.at[at, :], sem_w.at[n, p]) for p, at in enumerate(cuts)]
        )
    for copy in early:
        copy.start()
    for copy in early:
        copy.wait()
    for copy in late[0] + late[1]:
        copy.start()

    for n, pairs in enumerate((((0, (0, 1)), (1, (2, 3))), ((2, (0, 2)), (3, (1, 3))))):
        at = slice(n * step, n * step + step)
        summed = tok_in[at, :].astype(F32) + out_bias[...]
        for a, places in pairs:
            for m, r in enumerate(places):
                summed = summed + lax.dot_general(
                    att_in[a, m],
                    wo[r],
                    (((0,), (1,)), ((), ())),
                    preferred_element_type=F32,
                )
        total[at, :] = summed
        h[at, :] = norm(summed, gain[...], bias[...]).astype(BF16)

    for copy in late[0]:
        copy.wait()
    tile = 512

    @pl.loop(0, rows // step)
    def _(i):
        at = pl.ds(pl.multiple_of(i * step, step), step)
        for start in range(0, w1.shape[1], tile):
            cols = slice(start, start + tile)
            pre = jnp.dot(h[at, :], w1_in[:, cols], preferred_element_type=F32) + b1[:, cols]
            hidden[at, cols] = (0.5 * pre * (1.0 + lax.erf(pre * math.sqrt(0.5)))).astype(BF16)

    for place in range(4):

        @pl.when(me == place)
        def _(place=place):
            at = slice(place * quarter, place * quarter + quarter)
            mine[...] = (total[:, at] + b2[:, at]).T

    for copy in late[1]:
        copy.wait()

    @pl.loop(0, rows // step)
    def _(i):
        at = pl.ds(pl.multiple_of(i * step, step), step)
        total[at, :] = jnp.dot(hidden[at, :], w2_in[...], preferred_element_type=F32)

    for place in range(4):

        @pl.when(me == place)
        def _(place=place):
            mine[...] += total[:, place * quarter : place * quarter + quarter].T
            for r, ref in ((1, to1), (2, to2), (3, to3)):
                start = (place ^ r) * quarter
                ref[...] = total[:, start : start + quarter].T.astype(BF16)


def mlp(first, rows, where, slots, atts, wos, tok, out_bias, gain, bias, w1, b1, w2, b2):
    width = tok.shape[1]
    hidden = w1.shape[1]
    quarter = width // 4
    parts = 4
    return pl.pallas_call(
        functools.partial(mlp_kernel, first),
        in_specs=[SM] + [VM] * 5 + [ANY] * (3 + len(atts) + len(wos)),
        out_specs=[VM] * 4,
        out_shape=[jax.ShapeDtypeStruct((quarter, rows), F32)]
        + [jax.ShapeDtypeStruct((quarter, rows), BF16)] * 3,
        scratch_shapes=[
            pltpu.VMEM((rows, width), BF16),
            pltpu.VMEM((len(atts), *atts[0].shape), BF16),
            pltpu.VMEM(w1.shape, BF16),
            pltpu.VMEM(w2.shape, BF16),
            pltpu.VMEM((4, width, quarter), BF16),
            pltpu.VMEM((rows, width), F32),
            pltpu.VMEM((rows, width), BF16),
            pltpu.VMEM((rows, hidden), BF16),
            pltpu.SemaphoreType.DMA((len(atts) + 1,)),
            pltpu.SemaphoreType.DMA((2, 8, slots)),
            pltpu.SemaphoreType.DMA((2, parts)),
        ],
        compiler_params=params(52),
        cost_estimate=cost(2 * rows * width * (width + 2 * hidden), 25e6, rows * hidden),
        name="out_mlp",
    )(where, out_bias, gain, bias, b1, b2, tok, w1, w2, *atts, *wos)


def hold_kernel(where, own, other, wp, sems):
    folds, shard, _ = own.shape
    copies = []
    for k in range(folds):
        for n, src in enumerate((own, other)):
            start = pl.multiple_of((2 * k + (where[0] ^ n)) * shard, 16)
            copies.append(pltpu.make_async_copy(src.at[k], wp.at[pl.ds(start, shard), :], sems.at[n, k]))
    for copy in copies:
        copy.start()
    for copy in copies:
        copy.wait()


def hold(where, own, other):
    folds, shard, width = own.shape
    return pl.pallas_call(
        hold_kernel,
        in_specs=[SM, ANY, ANY],
        out_specs=VM,
        out_shape=jax.ShapeDtypeStruct((2 * folds * shard, width), BF16),
        scratch_shapes=[pltpu.SemaphoreType.DMA((2, folds))],
        compiler_params=params(48),
        cost_estimate=cost(0, 11e6),
        name="hold",
    )(where, own, other)


def project_kernel(folds, where, layer, stats, gain, bias, wp, mine, to1, to2, to3, acc):
    me = where[1]
    quarter = mine.shape[0]
    scale, shift = stats[0:1, :], stats[1:2, :]
    final = ((layer[...].astype(F32) - shift) * scale * gain[...] + bias[...]).astype(BF16)
    depth = wp.shape[0] // folds
    each = final.shape[1] // folds // CHUNKS
    for n in range(CHUNKS):
        part = 0.0
        for k in range(folds):
            start = (n * folds + k) * each
            part = part + lax.dot_general(
                final[:, start : start + each],
                wp[k * depth : k * depth + depth, :],
                (((0,), (0,)), ((), ())),
                preferred_element_type=F32,
            )
        acc[n * each : n * each + each, :] = part
    for place in range(4):

        @pl.when(me == place)
        def _(place=place):
            at = slice(place * quarter, place * quarter + quarter)
            mine[...] = acc[:, at].T
            for r, ref in ((1, to1), (2, to2), (3, to3)):
                first = (place ^ r) * quarter
                ref[...] = acc[:, first : first + quarter].T.astype(BF16)


def project(folds, where, layer, stats, gain, bias, wp):
    width = wp.shape[1]
    count = layer.shape[1] // folds
    quarter = width // 4
    return pl.pallas_call(
        functools.partial(project_kernel, folds),
        in_specs=[SM] + [VM] * 5,
        out_specs=[VM] * 4,
        out_shape=[jax.ShapeDtypeStruct((quarter, count), F32)]
        + [jax.ShapeDtypeStruct((quarter, count), BF16)] * 3,
        scratch_shapes=[pltpu.VMEM((count, width), F32)],
        compiler_params=params(16),
        cost_estimate=cost(2 * count * wp.size, 7e6),
        name="project",
    )(where, layer, stats, gain, bias, wp)


def gather_qkv(w_qkv, core):
    parts, shard, cols = w_qkv.shape
    count = lax.axis_size("tok")
    if shard % 16:
        whole = lax.all_gather(w_qkv, "tok", axis=1, tiled=True)
        low, high = whole[None, :, : whole.shape[1] // 2], whole[None, :, whole.shape[1] // 2 :]
        return jnp.where(core == 0, low, high), jnp.where(core == 0, high, low)
    own = lax.all_gather(
        w_qkv.reshape(parts * shard, cols), "tok", axis=0, tiled=True, axis_index_groups=same_core_groups(count)
    ).reshape(count // 2, parts, shard, cols)
    return own, None


def gather_proj_whole(w_proj, core):
    _, quarter = w_proj.shape
    whole = lax.all_gather(w_proj, "tok", axis=0, tiled=True).reshape(4, 4, quarter, quarter)
    whole = lax.all_to_all(whole, "blk", split_axis=1, concat_axis=3, tiled=True)
    whole = whole.reshape(4, 2, quarter // 2, 4 * quarter)
    low, high = whole[:, 0], whole[:, 1]
    return jnp.where(core == 0, low, high), jnp.where(core == 0, high, low)


def body(
    tokens,
    segment_ids,
    merge_index,
    segment_owner,
    ln1_gain,
    ln1_bias,
    w_qkv,
    qkv_bias,
    w_out,
    out_bias,
    ln2_gain,
    ln2_bias,
    w_fc1,
    fc1_bias,
    w_fc2,
    fc2_bias,
    ln3_gain,
    ln3_bias,
    w_proj,
    proj_bias,
):
    blk, tok = lax.axis_index("blk"), lax.axis_index("tok")
    core = tok % 2
    tok_count = lax.axis_size("tok")
    block = tokens[0]
    local_rows, width = block.shape
    rows = 4 * local_rows
    quarter = width // 4
    merges = merge_index[0]
    merged_count, folds = merges.shape

    half = local_rows // 2
    split_proj = w_proj.shape[0] == 2 * quarter and tok_count == 8
    even, low = (blk & 1) == 0, (blk & 2) == 0

    qkv_own, qkv_other = gather_qkv(w_qkv, core)
    a, b = block[:half], block[half:]
    depth, shard = w_out.shape
    if shard % 16:
        whole = lax.all_gather(w_out, "tok", axis=1, tiled=True).T
        shards = [lax.dynamic_slice_in_dim(whole, core * (width // 2), width // 2, 0)]
        where = jnp.stack([core, blk, core]).astype(jnp.int32)
    else:
        shards = [transpose(w_out)]
        shards += [swap(shards[0], "tok", 2 * n) for n in range(1, tok_count // 2)]
        where = jnp.stack([core, blk, tok]).astype(jnp.int32)
    xa, yb = swap(a, "blk", 1), swap(b, "blk", 2)
    xa, yb = stage(xa, yb)

    a, b = jnp.concatenate([a, xa], axis=0), jnp.concatenate([b, yb], axis=0)
    ya, xb = swap(a, "blk", 2), swap(b, "blk", 1)
    if split_proj:
        halves = stage(w_proj, a)[0].reshape(2, 2, quarter // 2, quarter)
        keep = jnp.where(core == 0, halves[:, 0], halves[:, 1])
        got = swap(jnp.where(core == 0, halves[:, 1], halves[:, 0]), "tok", 1)
        near = jnp.where((core == 0) == low, keep, got)
        far = jnp.where((core == 0) == low, got, keep)
        ya, xb, near, far = stage(ya, xb, near, far)
    else:
        ya, xb = stage(ya, xb)
    pieces = [a, ya, b, xb]

    ids = jnp.arange(rows, dtype=jnp.int32)
    seg_of = jnp.sum(jnp.where(merges[:, :1] == ids[None, :], segment_ids[0][None, :], 0), axis=1)
    owners = segment_owner[0]
    owner = jnp.sum(
        jnp.where(seg_of[:, None] == jnp.arange(owners.shape[0], dtype=jnp.int32)[None, :], owners[None, :], 0),
        axis=1,
    )
    order = jnp.arange(merged_count, dtype=jnp.int32)
    ahead = (owner[None, :] < owner[:, None]) | ((owner[None, :] == owner[:, None]) & (order[None, :] < order[:, None]))
    place = jnp.sum(ahead.astype(jnp.int32), axis=1)
    at_place = place[None, :] == order[:, None]
    owner_sorted = jnp.sum(jnp.where(at_place, owner[None, :], 0), axis=1)
    merges_sorted = jnp.sum(jnp.where(at_place[:, :, None], merges[None, :, :], 0), axis=1)
    chunks = CHUNKS
    count = merged_count // chunks
    perm = merges_sorted.reshape(chunks, count, folds).transpose(0, 2, 1).reshape(rows, 1)
    row_owner = jnp.broadcast_to(owner_sorted.reshape(chunks, 1, count), (chunks, folds, count)).reshape(rows)
    nth = ids // half
    swapped = (nth & 1) * 2 + (nth & 2) // 2
    device = jnp.where(nth < 4, nth, swapped) ^ blk
    source = device * local_rows + jnp.where(nth < 4, 0, half) + ids % half

    if split_proj:
        got, ya, xb = stage(swap(far, "blk", 2), ya, xb)
        pair = jnp.concatenate([jnp.where(low, near, got), jnp.where(low, got, near)], axis=2)
        keep, give = jnp.where(even, pair[0], pair[1]), jnp.where(even, pair[1], pair[0])
        pieces = [a, ya, b, xb]

    moved, normed = permute_norm(perm, source[None, :], pieces, ln1_gain[None, :], ln1_bias[None, :])
    if split_proj:
        got, moved, normed, *shards = stage(swap(give, "blk", 1), moved, normed, *shards)
    else:
        moved, normed, *shards = stage(moved, normed, *shards)

    slots = len(shards)
    shards = jnp.concatenate(shards, axis=0)
    a, b = shards[: width // 4], shards[width // 4 :]
    xa, yb = swap(a, "blk", 1), swap(b, "blk", 2)
    if split_proj:
        one, two = jnp.where(even, keep, got), jnp.where(even, got, keep)
        mine = jnp.concatenate([one[:, :quarter], two[:, :quarter], one[:, quarter:], two[:, quarter:]], axis=1)
        xa, yb, qkv_own, mine = stage(xa, yb, qkv_own, mine)
        proj_own = lax.all_gather(mine, "tok", axis=0, tiled=True, axis_index_groups=same_core_groups(tok_count))
        proj_own = proj_own.reshape(4, quarter // 2, width)
    else:
        xa, yb, qkv_own = stage(xa, yb, qkv_own)
        proj_own, proj_other = gather_proj_whole(w_proj, core)

    a, b = jnp.stack([a, xa]), jnp.stack([b, yb])
    ya, xb = swap(a, "blk", 2), swap(b, "blk", 1)
    if qkv_other is None:
        qkv_other = swap(qkv_own, "tok", 1)
    chunk_rows = rows // chunks
    a0, b0, a1, b1 = qkv_attend(
        where, normed, qkv_own, qkv_other, qkv_bias, row_owner[:, None], row_owner[None, :]
    )
    a0, b0, a1, b1, ya, xb = stage(a0, b0, a1, b1, ya, xb)

    wos = [a, ya, b, xb]
    wos += [swap(x, "tok", 1) for x in wos]
    xa0, yb0 = swap(a0, "blk", 1), swap(b0, "blk", 2)
    xa0, yb0, a1, b1, *wos = stage(xa0, yb0, a1, b1, *wos)

    a0, b0 = jnp.stack([a0, xa0]), jnp.stack([b0, yb0])
    ya0, xb0 = swap(a0, "blk", 2), swap(b0, "blk", 1)
    xa1, yb1 = swap(a1, "blk", 1), swap(b1, "blk", 2)
    gain3 = lax.dynamic_slice_in_dim(ln3_gain, blk * quarter, quarter, 0)
    bias3 = lax.dynamic_slice_in_dim(ln3_bias, blk * quarter, quarter, 0)
    a0, ya0, b0, xb0, xa1, yb1, gain3, bias3 = stage(a0, ya0, b0, xb0, xa1, yb1, gain3, bias3)
    a1, b1 = jnp.stack([a1, xa1]), jnp.stack([b1, yb1])
    ya1, xb1 = swap(a1, "blk", 2), swap(b1, "blk", 1)

    def dense(atts, n):
        return mlp(
            n * chunk_rows, chunk_rows, where, slots, atts, wos, moved, out_bias[None, :],
            ln2_gain[None, :], ln2_bias[None, :], w_fc1, fc1_bias[None, :], w_fc2, fc2_bias[None, :],
        )

    own0, *sends0 = dense([a0, ya0, b0, xb0], 0)
    own0, *sends0, a1, ya1, b1, xb1 = stage(own0, *sends0, a1, ya1, b1, xb1)
    if split_proj:
        proj_own, own0 = stage(proj_own, own0)
        proj_other = swap(proj_own, "tok", 1)
    parts0 = [swap(x, "blk", r) for r, x in enumerate(sends0, 1)]
    own1, *sends1 = dense([a1, ya1, b1, xb1], 1)
    own1, proj_other, *rest = stage(own1, proj_other, *sends1, *parts0)
    sends1, parts0 = rest[:3], rest[3:]
    parts1 = [swap(x, "blk", r) for r, x in enumerate(sends1, 1)]

    wp = hold(where, proj_own, proj_other)
    *parts1, wp = stage(*parts1, wp)
    own = jnp.concatenate([own0, own1], axis=1)
    for x0, x1 in zip(parts0, parts1):
        own = own + jnp.concatenate([x0, x1], axis=1).astype(F32)
    layer = own.astype(BF16)
    wide = layer.astype(F32)
    mean = jnp.mean(wide, axis=0)
    centered = wide - mean[None, :]
    spread = jnp.sum(centered * centered, axis=0)
    seen = quarter
    for r in (1, 2):
        other = swap(jnp.stack([mean, spread]), "blk", r)
        spread = spread + other[1] + (mean - other[0]) ** 2 * (seen / 2)
        mean = (mean + other[0]) * 0.5
        seen *= 2
    stats = jnp.stack([lax.rsqrt(spread / width + EPS), mean])
    own, *sends = project(folds, where, layer, stats, gain3[:, None], bias3[:, None], wp)
    for r, x in enumerate(sends, 1):
        own = own + swap(x, "blk", r).astype(F32)
    projected = (own + proj_bias[:, None]).astype(BF16)

    slot_cap = 2 * merged_count // tok_count
    first = jnp.sum((owner_sorted[None, :] < owner_sorted[:, None]).astype(jnp.int32), axis=1)
    target = owner_sorted * slot_cap + order - first
    placed = (jnp.arange(tok_count * slot_cap, dtype=jnp.int32)[:, None] == target[None, :]).astype(BF16)
    outgoing = lax.dot_general(placed, projected, (((1,), (1,)), ((), ())), preferred_element_type=F32).astype(BF16)
    outgoing = outgoing.reshape(tok_count, slot_cap, quarter)
    arrived = lax.all_to_all(outgoing, "tok", split_axis=0, concat_axis=0, tiled=True)
    return arrived[None]


def solution(mesh):
    placed = (
        P("tok", "blk", None),
        P("tok", None),
        P("tok", None, None),
        P("tok", None),
        P(),
        P(),
        P(None, "tok", "blk"),
        P(None, "blk"),
        P("blk", "tok"),
        P(),
        P(),
        P(),
        P(None, "blk"),
        P("blk"),
        P("blk", None),
        P(),
        P(),
        P(),
        P("tok", "blk"),
        P("blk"),
    )
    return jax.shard_map(
        body, mesh=mesh, in_specs=placed, out_specs=P("tok", None, None, "blk"), check_vma=False
    )
```

```python
import functools
import math

import jax
import jax.numpy as jnp
from jax import lax
from jax.experimental import pallas as pl
from jax.experimental.pallas import tpu as pltpu
from jax.sharding import PartitionSpec as P

HD = 104
EPS = 1e-06
CHUNKS = 2
BF16 = jnp.bfloat16
F32 = jnp.float32
VM = pl.BlockSpec(memory_space=pltpu.VMEM)
SM = pl.BlockSpec(memory_space=pltpu.SMEM)
ANY = pl.BlockSpec(memory_space=pl.ANY)


def cost(flops, nbytes, trans=0):
    return pl.CostEstimate(flops=int(flops), bytes_accessed=int(nbytes), transcendentals=int(trans))


def params(mib):
    return pltpu.CompilerParams(vmem_limit_bytes=mib * 1024 * 1024)


def norm(x, gain, bias):
    center = x - jnp.mean(x, axis=-1, keepdims=True)
    spread = jnp.mean(center * center, axis=-1, keepdims=True)
    return center * lax.rsqrt(spread + EPS) * gain + bias


def swap(x, axis, mask):
    return lax.ppermute(x, axis, [(i, i ^ mask) for i in range(lax.axis_size(axis))])


def stage(*arrays):
    return lax.optimization_barrier(arrays)


def same_core_groups(count):
    return [list(range(core, count, 2)) for core in range(2)]


def permute_norm_kernel(count, perm, place, gain, bias, *refs):
    pieces, (moved, normed, tok, sems) = refs[:count], refs[count:]

    @pl.when(pl.program_id(0) == 0)
    def _():
        copies, start = [], 0
        for n, piece in enumerate(pieces):
            size = piece.shape[0]
            copies.append(pltpu.make_async_copy(piece, tok.at[pl.ds(start, size), :], sems.at[n]))
            start += size
        for copy in copies:
            copy.start()
        for copy in copies:
            copy.wait()

    pick = (perm[...] == place[...]).astype(F32).astype(BF16)
    rows = jnp.dot(pick, tok[...], preferred_element_type=F32)
    moved[...] = rows.astype(BF16)
    normed[...] = norm(rows, gain[...], bias[...]).astype(BF16)


def permute_norm(perm, place, pieces, gain, bias):
    rows, width = perm.shape[0], pieces[0].shape[1]
    step = 256
    return pl.pallas_call(
        functools.partial(permute_norm_kernel, len(pieces)),
        grid=(rows // step,),
        in_specs=[
            pl.BlockSpec((step, 1), lambda i: (i, 0)),
            pl.BlockSpec((1, rows), lambda i: (0, 0)),
            pl.BlockSpec((1, width), lambda i: (0, 0)),
            pl.BlockSpec((1, width), lambda i: (0, 0)),
        ]
        + [ANY] * len(pieces),
        out_specs=[pl.BlockSpec((step, width), lambda i: (i, 0))] * 2,
        out_shape=[jax.ShapeDtypeStruct((rows, width), BF16)] * 2,
        scratch_shapes=[pltpu.VMEM((rows, width), BF16), pltpu.SemaphoreType.DMA((len(pieces),))],
        compiler_params=params(56),
        cost_estimate=cost(2 * rows * rows * width, 6 * rows * width),
        name="permute_norm",
    )(perm, place, gain, bias, *pieces)


def transpose_kernel(x, out):
    out[...] = x[...].T


def transpose(x):
    return pl.pallas_call(
        transpose_kernel,
        in_specs=[VM],
        out_specs=VM,
        out_shape=jax.ShapeDtypeStruct(x.shape[::-1], x.dtype),
        compiler_params=params(8),
        cost_estimate=cost(0, 4 * x.size),
        name="transpose",
    )(x)


def attend_rows(first, qkv, row_owner, col_owner, *outs):
    cols, step = outs[0].shape
    scale = math.log2(math.e) / math.sqrt(HD)
    keys = qkv.shape[1]
    for head in range(cols // HD):
        at = slice(head * HD, head * HD + HD)
        key = qkv[1, :, at]
        value = jnp.concatenate([qkv[2, :, at], jnp.ones((keys, 128 - HD), BF16)], axis=1)
        for n, out in enumerate(outs):
            start = n * step
            mine = slice(start, start + step)
            query = qkv[0, first + start : first + start + step, at]
            scores = lax.dot_general(query, key, (((1,), (1,)), ((), ())), preferred_element_type=F32)
            kept = row_owner[mine, :] == col_owner[...]
            scores = jnp.where(kept, scores, -1e30)
            weights = jnp.exp2((scores - jnp.max(scores, axis=1, keepdims=True)) * scale).astype(BF16)
            mixed = jnp.dot(weights, value, preferred_element_type=F32)
            out[at, :] = (mixed / mixed[:, HD : HD + 1]).T[:HD, :].astype(BF16)


def qkv_attend_kernel(core, h, own, other, bias, row_owner, col_owner, *refs):
    *outs, out, weight, sems = refs
    groups, _, shard, _ = own.shape
    me = core[0]
    copies = []
    for z in range(groups):
        for n, (src, c) in enumerate(((own, me), (other, 1 - me))):
            start = pl.multiple_of((2 * z + c) * shard, 16)
            copy = pltpu.make_async_copy(src.at[z], weight.at[:, pl.ds(start, shard), :], sems.at[n, z])
            copy.start()
            copies.append(copy)
    for copy in copies:
        copy.wait()
    rows = h.shape[0]
    step = 256

    for part in range(3):

        @pl.loop(0, rows // step)
        def _(i):
            at = pl.ds(pl.multiple_of(i * step, step), step)
            acc = jnp.dot(h[at, :], weight[part], preferred_element_type=F32)
            out[part, at, :] = (acc + bias[part : part + 1, :]).astype(BF16)

    chunk = rows // CHUNKS
    for n in range(CHUNKS):
        attend_rows(n * chunk, out, row_owner.at[n * chunk : n * chunk + chunk, :], col_owner, *outs[2 * n : 2 * n + 2])


def qkv_attend(core, h, own, other, bias, row_owner, col_owner):
    groups, parts, shard, cols = own.shape
    rows, width = h.shape
    return pl.pallas_call(
        qkv_attend_kernel,
        in_specs=[SM, VM, ANY, ANY, VM, VM, VM],
        out_specs=[VM] * (2 * CHUNKS),
        out_shape=[jax.ShapeDtypeStruct((cols, rows // CHUNKS // 2), BF16)] * (2 * CHUNKS),
        scratch_shapes=[
            pltpu.VMEM((parts, rows, cols), BF16),
            pltpu.VMEM((parts, width, cols), BF16),
            pltpu.SemaphoreType.DMA((2, groups)),
        ],
        compiler_params=params(32),
        cost_estimate=cost(2 * rows * width * parts * cols + 4 * rows * rows * cols, 16e6, rows * rows * (cols // HD)),
        name="qkv_attend",
    )(core, h, own, other, bias, row_owner, col_owner)


def mlp_kernel(first, where, out_bias, gain, bias, b1, b2, tok, w1, w2, *refs):
    atts, wos, (mine, to1, to2, to3, *scratch) = refs[:4], refs[4:12], refs[12:]
    tok_in, att_in, w1_in, w2_in, wo, total, h, hidden, sem_a, sem_o, sem_w = scratch
    core, me = where[0], where[1]
    quarter, rows = mine.shape
    step = rows // 2
    early = [pltpu.make_async_copy(tok.at[first : first + rows, :], tok_in, sem_a.at[4])]
    for n, src in enumerate(atts):
        early.append(pltpu.make_async_copy(src, att_in.at[n], sem_a.at[n]))
    count, slots = wos[0].shape[1], sem_o.shape[2]
    size = min(count, wo.shape[1] // 2 // slots)
    for n in range(2):
        for m, r in enumerate((0, 1, 2, 3, 0, 2, 1, 3)):
            for p in range(count // size):
                row = (m // 4) * count + p * size
                slot, off = divmod(row, wo.shape[1] // 2 // slots)
                place = (where[2] ^ (2 * slot) ^ n) * (wo.shape[1] // 2 // slots) + off
                start = pl.multiple_of(place, 16)
                early.append(
                    pltpu.make_async_copy(
                        wos[4 * n + m // 2].at[m % 2, p * size : p * size + size, :],
                        wo.at[r, pl.ds(start, size), :],
                        sem_o.at[n, m, p],
                    )
                )
    parts = sem_w.shape[1]
    late = []
    for n, (src, dst) in enumerate(((w1, w1_in), (w2, w2_in))):
        size = src.shape[0] // parts
        cuts = [slice(p * size, p * size + size) for p in range(parts)]
        late.append(
            [pltpu.make_async_copy(src.at[at, :], dst.at[at, :], sem_w.at[n, p]) for p, at in enumerate(cuts)]
        )
    for copy in early:
        copy.start()
    for copy in early:
        copy.wait()
    for copy in late[0] + late[1]:
        copy.start()

    for n, pairs in enumerate((((0, (0, 1)), (1, (2, 3))), ((2, (0, 2)), (3, (1, 3))))):
        at = slice(n * step, n * step + step)
        summed = tok_in[at, :].astype(F32) + out_bias[...]
        for a, places in pairs:
            for m, r in enumerate(places):
                summed = summed + lax.dot_general(
                    att_in[a, m],
                    wo[r],
                    (((0,), (1,)), ((), ())),
                    preferred_element_type=F32,
                )
        total[at, :] = summed
        h[at, :] = norm(summed, gain[...], bias[...]).astype(BF16)

    for copy in late[0]:
        copy.wait()
    tile = 512

    @pl.loop(0, rows // step)
    def _(i):
        at = pl.ds(pl.multiple_of(i * step, step), step)
        for start in range(0, w1.shape[1], tile):
            cols = slice(start, start + tile)
            pre = jnp.dot(h[at, :], w1_in[:, cols], preferred_element_type=F32) + b1[:, cols]
            hidden[at, cols] = (0.5 * pre * (1.0 + lax.erf(pre * math.sqrt(0.5)))).astype(BF16)

    for place in range(4):

        @pl.when(me == place)
        def _(place=place):
            at = slice(place * quarter, place * quarter + quarter)
            mine[...] = (total[:, at] + b2[:, at]).T

    for copy in late[1]:
        copy.wait()

    @pl.loop(0, rows // step)
    def _(i):
        at = pl.ds(pl.multiple_of(i * step, step), step)
        total[at, :] = jnp.dot(hidden[at, :], w2_in[...], preferred_element_type=F32)

    for place in range(4):

        @pl.when(me == place)
        def _(place=place):
            mine[...] += total[:, place * quarter : place * quarter + quarter].T
            for r, ref in ((1, to1), (2, to2), (3, to3)):
                start = (place ^ r) * quarter
                ref[...] = total[:, start : start + quarter].T.astype(BF16)


def mlp(first, rows, where, slots, atts, wos, tok, out_bias, gain, bias, w1, b1, w2, b2):
    width = tok.shape[1]
    hidden = w1.shape[1]
    quarter = width // 4
    parts = 4
    return pl.pallas_call(
        functools.partial(mlp_kernel, first),
        in_specs=[SM] + [VM] * 5 + [ANY] * (3 + len(atts) + len(wos)),
        out_specs=[VM] * 4,
        out_shape=[jax.ShapeDtypeStruct((quarter, rows), F32)]
        + [jax.ShapeDtypeStruct((quarter, rows), BF16)] * 3,
        scratch_shapes=[
            pltpu.VMEM((rows, width), BF16),
            pltpu.VMEM((len(atts), *atts[0].shape), BF16),
            pltpu.VMEM(w1.shape, BF16),
            pltpu.VMEM(w2.shape, BF16),
            pltpu.VMEM((4, width, quarter), BF16),
            pltpu.VMEM((rows, width), F32),
            pltpu.VMEM((rows, width), BF16),
            pltpu.VMEM((rows, hidden), BF16),
            pltpu.SemaphoreType.DMA((len(atts) + 1,)),
            pltpu.SemaphoreType.DMA((2, 8, slots)),
            pltpu.SemaphoreType.DMA((2, parts)),
        ],
        compiler_params=params(52),
        cost_estimate=cost(2 * rows * width * (width + 2 * hidden), 25e6, rows * hidden),
        name="out_mlp",
    )(where, out_bias, gain, bias, b1, b2, tok, w1, w2, *atts, *wos)


def hold_kernel(where, own, other, wp, sems):
    folds, shard, _ = own.shape
    copies = []
    for k in range(folds):
        for n, src in enumerate((own, other)):
            start = pl.multiple_of((2 * k + (where[0] ^ n)) * shard, 16)
            copies.append(pltpu.make_async_copy(src.at[k], wp.at[pl.ds(start, shard), :], sems.at[n, k]))
    for copy in copies:
        copy.start()
    for copy in copies:
        copy.wait()


def hold(where, own, other):
    folds, shard, width = own.shape
    return pl.pallas_call(
        hold_kernel,
        in_specs=[SM, ANY, ANY],
        out_specs=VM,
        out_shape=jax.ShapeDtypeStruct((2 * folds * shard, width), BF16),
        scratch_shapes=[pltpu.SemaphoreType.DMA((2, folds))],
        compiler_params=params(48),
        cost_estimate=cost(0, 11e6),
        name="hold",
    )(where, own, other)


def project_kernel(folds, where, layer, stats, gain, bias, wp, mine, to1, to2, to3, acc):
    me = where[1]
    quarter = mine.shape[0]
    scale, shift = stats[0:1, :], stats[1:2, :]
    final = ((layer[...].astype(F32) - shift) * scale * gain[...] + bias[...]).astype(BF16)
    depth = wp.shape[0] // folds
    each = final.shape[1] // folds // CHUNKS
    for n in range(CHUNKS):
        part = 0.0
        for k in range(folds):
            start = (n * folds + k) * each
            part = part + lax.dot_general(
                final[:, start : start + each],
                wp[k * depth : k * depth + depth, :],
                (((0,), (0,)), ((), ())),
                preferred_element_type=F32,
            )
        acc[n * each : n * each + each, :] = part
    for place in range(4):

        @pl.when(me == place)
        def _(place=place):
            at = slice(place * quarter, place * quarter + quarter)
            mine[...] = acc[:, at].T
            for r, ref in ((1, to1), (2, to2), (3, to3)):
                first = (place ^ r) * quarter
                ref[...] = acc[:, first : first + quarter].T.astype(BF16)


def project(folds, where, layer, stats, gain, bias, wp):
    width = wp.shape[1]
    count = layer.shape[1] // folds
    quarter = width // 4
    return pl.pallas_call(
        functools.partial(project_kernel, folds),
        in_specs=[SM] + [VM] * 5,
        out_specs=[VM] * 4,
        out_shape=[jax.ShapeDtypeStruct((quarter, count), F32)]
        + [jax.ShapeDtypeStruct((quarter, count), BF16)] * 3,
        scratch_shapes=[pltpu.VMEM((count, width), F32)],
        compiler_params=params(16),
        cost_estimate=cost(2 * count * wp.size, 7e6),
        name="project",
    )(where, layer, stats, gain, bias, wp)


def gather_qkv(w_qkv, core):
    parts, shard, cols = w_qkv.shape
    count = lax.axis_size("tok")
    if shard % 16:
        whole = lax.all_gather(w_qkv, "tok", axis=1, tiled=True)
        low, high = whole[None, :, : whole.shape[1] // 2], whole[None, :, whole.shape[1] // 2 :]
        return jnp.where(core == 0, low, high), jnp.where(core == 0, high, low)
    own = lax.all_gather(
        w_qkv.reshape(parts * shard, cols), "tok", axis=0, tiled=True, axis_index_groups=same_core_groups(count)
    ).reshape(count // 2, parts, shard, cols)
    return own, None


def gather_proj_whole(w_proj, core):
    _, quarter = w_proj.shape
    whole = lax.all_gather(w_proj, "tok", axis=0, tiled=True).reshape(4, 4, quarter, quarter)
    whole = lax.all_to_all(whole, "blk", split_axis=1, concat_axis=3, tiled=True)
    whole = whole.reshape(4, 2, quarter // 2, 4 * quarter)
    low, high = whole[:, 0], whole[:, 1]
    return jnp.where(core == 0, low, high), jnp.where(core == 0, high, low)


def body(
    tokens,
    segment_ids,
    merge_index,
    segment_owner,
    ln1_gain,
    ln1_bias,
    w_qkv,
    qkv_bias,
    w_out,
    out_bias,
    ln2_gain,
    ln2_bias,
    w_fc1,
    fc1_bias,
    w_fc2,
    fc2_bias,
    ln3_gain,
    ln3_bias,
    w_proj,
    proj_bias,
):
    blk, tok = lax.axis_index("blk"), lax.axis_index("tok")
    core = tok % 2
    tok_count = lax.axis_size("tok")
    block = tokens[0]
    local_rows, width = block.shape
    rows = 4 * local_rows
    quarter = width // 4
    merges = merge_index[0]
    merged_count, folds = merges.shape

    half = local_rows // 2
    split_proj = w_proj.shape[0] == 2 * quarter and tok_count == 8
    even, low = (blk & 1) == 0, (blk & 2) == 0

    qkv_own, qkv_other = gather_qkv(w_qkv, core)
    a, b = block[:half], block[half:]
    depth, shard = w_out.shape
    if shard % 16:
        whole = lax.all_gather(w_out, "tok", axis=1, tiled=True).T
        shards = [lax.dynamic_slice_in_dim(whole, core * (width // 2), width // 2, 0)]
        where = jnp.stack([core, blk, core]).astype(jnp.int32)
    else:
        shards = [transpose(w_out)]
        shards += [swap(shards[0], "tok", 2 * n) for n in range(1, tok_count // 2)]
        where = jnp.stack([core, blk, tok]).astype(jnp.int32)
    xa, yb = swap(a, "blk", 1), swap(b, "blk", 2)
    xa, yb = stage(xa, yb)

    a, b = jnp.concatenate([a, xa], axis=0), jnp.concatenate([b, yb], axis=0)
    ya, xb = swap(a, "blk", 2), swap(b, "blk", 1)
    if split_proj:
        halves = stage(w_proj, a)[0].reshape(2, 2, quarter // 2, quarter)
        keep = jnp.where(core == 0, halves[:, 0], halves[:, 1])
        got = swap(jnp.where(core == 0, halves[:, 1], halves[:, 0]), "tok", 1)
        near = jnp.where((core == 0) == low, keep, got)
        far = jnp.where((core == 0) == low, got, keep)
        ya, xb, near, far = stage(ya, xb, near, far)
    else:
        ya, xb = stage(ya, xb)
    pieces = [a, ya, b, xb]

    ids = jnp.arange(rows, dtype=jnp.int32)
    seg_of = jnp.sum(jnp.where(merges[:, :1] == ids[None, :], segment_ids[0][None, :], 0), axis=1)
    owners = segment_owner[0]
    owner = jnp.sum(
        jnp.where(seg_of[:, None] == jnp.arange(owners.shape[0], dtype=jnp.int32)[None, :], owners[None, :], 0),
        axis=1,
    )
    order = jnp.arange(merged_count, dtype=jnp.int32)
    ahead = (owner[None, :] < owner[:, None]) | ((owner[None, :] == owner[:, None]) & (order[None, :] < order[:, None]))
    place = jnp.sum(ahead.astype(jnp.int32), axis=1)
    at_place = place[None, :] == order[:, None]
    owner_sorted = jnp.sum(jnp.where(at_place, owner[None, :], 0), axis=1)
    merges_sorted = jnp.sum(jnp.where(at_place[:, :, None], merges[None, :, :], 0), axis=1)
    chunks = CHUNKS
    count = merged_count // chunks
    perm = merges_sorted.reshape(chunks, count, folds).transpose(0, 2, 1).reshape(rows, 1)
    row_owner = jnp.broadcast_to(owner_sorted.reshape(chunks, 1, count), (chunks, folds, count)).reshape(rows)
    nth = ids // half
    swapped = (nth & 1) * 2 + (nth & 2) // 2
    device = jnp.where(nth < 4, nth, swapped) ^ blk
    source = device * local_rows + jnp.where(nth < 4, 0, half) + ids % half

    if split_proj:
        got, ya, xb = stage(swap(far, "blk", 2), ya, xb)
        pair = jnp.concatenate([jnp.where(low, near, got), jnp.where(low, got, near)], axis=2)
        keep, give = jnp.where(even, pair[0], pair[1]), jnp.where(even, pair[1], pair[0])
        pieces = [a, ya, b, xb]

    moved, normed = permute_norm(perm, source[None, :], pieces, ln1_gain[None, :], ln1_bias[None, :])
    if split_proj:
        got, moved, normed, *shards = stage(swap(give, "blk", 1), moved, normed, *shards)
    else:
        moved, normed, *shards = stage(moved, normed, *shards)

    slots = len(shards)
    shards = jnp.concatenate(shards, axis=0)
    a, b = shards[: width // 4], shards[width // 4 :]
    xa, yb = swap(a, "blk", 1), swap(b, "blk", 2)
    if split_proj:
        one, two = jnp.where(even, keep, got), jnp.where(even, got, keep)
        mine = jnp.concatenate([one[:, :quarter], two[:, :quarter], one[:, quarter:], two[:, quarter:]], axis=1)
        xa, yb, qkv_own, mine = stage(xa, yb, qkv_own, mine)
        proj_own = lax.all_gather(mine, "tok", axis=0, tiled=True, axis_index_groups=same_core_groups(tok_count))
        proj_own = proj_own.reshape(4, quarter // 2, width)
    else:
        xa, yb, qkv_own = stage(xa, yb, qkv_own)
        proj_own, proj_other = gather_proj_whole(w_proj, core)

    a, b = jnp.stack([a, xa]), jnp.stack([b, yb])
    ya, xb = swap(a, "blk", 2), swap(b, "blk", 1)
    if qkv_other is None:
        qkv_other = swap(qkv_own, "tok", 1)
    chunk_rows = rows // chunks
    a0, b0, a1, b1 = qkv_attend(
        where, normed, qkv_own, qkv_other, qkv_bias, row_owner[:, None], row_owner[None, :]
    )
    a0, b0, a1, b1, ya, xb = stage(a0, b0, a1, b1, ya, xb)

    wos = [a, ya, b, xb]
    wos += [swap(x, "tok", 1) for x in wos]
    xa0, yb0 = swap(a0, "blk", 1), swap(b0, "blk", 2)
    xa0, yb0, a1, b1, *wos = stage(xa0, yb0, a1, b1, *wos)

    a0, b0 = jnp.stack([a0, xa0]), jnp.stack([b0, yb0])
    ya0, xb0 = swap(a0, "blk", 2), swap(b0, "blk", 1)
    xa1, yb1 = swap(a1, "blk", 1), swap(b1, "blk", 2)
    gain3 = lax.dynamic_slice_in_dim(ln3_gain, blk * quarter, quarter, 0)
    bias3 = lax.dynamic_slice_in_dim(ln3_bias, blk * quarter, quarter, 0)
    a0, ya0, b0, xb0, xa1, yb1, gain3, bias3 = stage(a0, ya0, b0, xb0, xa1, yb1, gain3, bias3)
    a1, b1 = jnp.stack([a1, xa1]), jnp.stack([b1, yb1])
    ya1, xb1 = swap(a1, "blk", 2), swap(b1, "blk", 1)

    def dense(atts, n):
        return mlp(
            n * chunk_rows, chunk_rows, where, slots, atts, wos, moved, out_bias[None, :],
            ln2_gain[None, :], ln2_bias[None, :], w_fc1, fc1_bias[None, :], w_fc2, fc2_bias[None, :],
        )

    own0, *sends0 = dense([a0, ya0, b0, xb0], 0)
    own0, *sends0, a1, ya1, b1, xb1 = stage(own0, *sends0, a1, ya1, b1, xb1)
    if split_proj:
        proj_own, own0 = stage(proj_own, own0)
        proj_other = swap(proj_own, "tok", 1)
    parts0 = [swap(x, "blk", r) for r, x in enumerate(sends0, 1)]
    own1, *sends1 = dense([a1, ya1, b1, xb1], 1)
    own1, proj_other, *rest = stage(own1, proj_other, *sends1, *parts0)
    sends1, parts0 = rest[:3], rest[3:]
    parts1 = [swap(x, "blk", r) for r, x in enumerate(sends1, 1)]

    wp = hold(where, proj_own, proj_other)
    *parts1, wp = stage(*parts1, wp)
    own = jnp.concatenate([own0, own1], axis=1)
    for x0, x1 in zip(parts0, parts1):
        own = own + jnp.concatenate([x0, x1], axis=1).astype(F32)
    layer = own.astype(BF16)
    wide = layer.astype(F32)
    mean = jnp.mean(wide, axis=0)
    centered = wide - mean[None, :]
    spread = jnp.sum(centered * centered, axis=0)
    seen = quarter
    for r in (1, 2):
        other = swap(jnp.stack([mean, spread]), "blk", r)
        spread = spread + other[1] + (mean - other[0]) ** 2 * (seen / 2)
        mean = (mean + other[0]) * 0.5
        seen *= 2
    stats = jnp.stack([lax.rsqrt(spread / width + EPS), mean])
    own, *sends = project(folds, where, layer, stats, gain3[:, None], bias3[:, None], wp)
    for r, x in enumerate(sends, 1):
        own = own + swap(x, "blk", r).astype(F32)
    projected = (own + proj_bias[:, None]).astype(BF16)

    slot_cap = 2 * merged_count // tok_count
    first = jnp.sum((owner_sorted[None, :] < owner_sorted[:, None]).astype(jnp.int32), axis=1)
    target = owner_sorted * slot_cap + order - first
    placed = (jnp.arange(tok_count * slot_cap, dtype=jnp.int32)[:, None] == target[None, :]).astype(BF16)
    outgoing = lax.dot_general(placed, projected, (((1,), (1,)), ((), ())), preferred_element_type=F32).astype(BF16)
    outgoing = outgoing.reshape(tok_count, slot_cap, quarter)
    arrived = lax.all_to_all(outgoing, "tok", split_axis=0, concat_axis=0, tiled=True)
    return arrived[None]


def solution(mesh):
    placed = (
        P("tok", "blk", None),
        P("tok", None),
        P("tok", None, None),
        P("tok", None),
        P(),
        P(),
        P(None, "tok", "blk"),
        P(None, "blk"),
        P("blk", "tok"),
        P(),
        P(),
        P(),
        P(None, "blk"),
        P("blk"),
        P("blk", None),
        P(),
        P(),
        P(),
        P("tok", "blk"),
        P("blk"),
    )
    return jax.shard_map(
        body, mesh=mesh, in_specs=placed, out_specs=P("tok", None, None, "blk"), check_vma=False
    )
```
